128 devices in a mesh: ctx: 8 (over x, z_lo), tp: 16 (over z_hi, y, core).
Axes of the slice: x: 4, y: 4, z: 4 (z_hi: 2, z_lo: 2; z = z_hi * 2 + z_lo), core: 2. Of those that a mesh axis runs over, the one named last changes fastest.
Arguments:
- queries: bfloat16 [8192, 2048], P('ctx', 'tp'), may hold values from -6 to 6
- keys: bfloat16 [8192, 128], P(('ctx', 'tp')), may hold values from -6 to 6
- values: bfloat16 [8192, 128], P(('ctx', 'tp')), may hold values from -6 to 6
- outputs: bfloat16 [8192, 2048], P('ctx', 'tp'), may hold values from -6 to 6
- out_grad: bfloat16 [8192, 2048], P('ctx', 'tp'), may hold values from -6 to 6
- log_norm: float32 [16, 8192], P('tp', 'ctx'), may hold values from 4 to 6
- doc_ids: int32 [8192], replicated, may hold values from 0 to 7, never falling along the last dimension, each value on 1 to 5120 neighbouring positions
Outputs:
- query_grad: bfloat16 [8192, 2048], P('ctx', 'tp')
- key_grad: bfloat16 [8192, 128], P(('ctx', 'tp'))
- value_grad: bfloat16 [8192, 128], P(('ctx', 'tp'))
The draws below stay inside these ranges and needn't reach their ends.
Inputs may be any that keep to these rules, and one draw needn't show every extreme that they name: `doc_ids`: document numbers never fall along the positions; each document has 1 to 5120 positions, one exactly that many.
All inputs are finite; a program needn't handle non-finite values.
Results may differ from the reference program's by a relative error of at most 0.006.
Values may be sent and summed in bfloat16 or wider, within the bound.
A program may use at most 64 MiB of HBM per device.

```python
import math
import jax
import jax.numpy as jnp
import numpy as np
from jax import lax

HD = 128
TOK_DEV = 1024
HEADS = 16
SEQ = 8192
N_CTX = 8


def level_of(own_key, dims, split, smallest, high):
    gain = 1.0
    for axis_at, blocks in split:
        steps = jax.random.uniform(jax.random.fold_in(jax.random.fold_in(own_key, 6), axis_at), (blocks,), jnp.float32, smallest / len(split), high / len(split))
        gain = gain * jnp.repeat(jnp.exp(steps), dims[axis_at] // blocks).reshape((-1,) + (1,) * (len(dims) - 1 - axis_at))
    return gain


def profile(count, total, most, skew):
    weights = [(1 << 20) // math.isqrt(rank ** skew) + 1 for rank in range(2, count + 1)]
    spare, counts = total - most - (count - 1), [1] * (count - 1)
    while spare > 0:
        movable = [i for i in range(count - 1) if counts[i] < most]
        pool, budget = sum([weights[i] for i in movable]), spare
        for i in movable:
            more = min(most - counts[i], max(1, budget * weights[i] // pool), spare)
            counts[i] = counts[i] + more
            spare = spare - more
    return np.array([most] + counts)


def uneven(stream_key, count, total, bound, skew):
    if count == 2:
        one = jax.random.randint(stream_key, (), max(1, total - bound), min(bound, total - 1) + 1)
        return jnp.stack([one, total - one])
    tallies = jnp.asarray(profile(count, total, bound, skew), jnp.int32)
    twos = (count - 1) // 2
    source_of, sink = tallies[1:1 + 2 * twos:2], tallies[2:2 + 2 * twos:2]
    margin = jnp.minimum(source_of - 1, bound - sink)
    shifted = jax.random.randint(jax.random.fold_in(stream_key, 1), (twos,), 0, 1 << 20) % (margin + 1)
    tallies = tallies.at[1:1 + 2 * twos:2].set(source_of - shifted).at[2:2 + 2 * twos:2].set(sink + shifted)
    return tallies[jax.random.permutation(jax.random.fold_in(stream_key, 2), count)]


def bell_draw(stream_key, extent, spread, limit, split=(), kind=jnp.bfloat16):
    result = spread * jax.random.normal(stream_key, extent, jnp.float32)
    if split:
        result = result * level_of(stream_key, extent, split, -0.22, 0.18)
    return jnp.clip(result, -limit, limit).astype(kind)


def setup_inputs(seed: int = 0) -> dict:
    splits = jax.random.split(jax.random.key(seed), 8)
    queries = bell_draw(splits[0], (SEQ, HEADS * HD), 1.0, 6.0, ((0, 8), (1, 16)))
    keys = bell_draw(splits[1], (SEQ, HD), 1.0, 6.0, ((0, 128),))
    values = bell_draw(splits[2], (SEQ, HD), 1.0, 6.0, ((0, 128),))
    outputs = bell_draw(splits[3], (SEQ, HEADS * HD), 1.0, 6.0, ((0, 8), (1, 16)))
    out_grad = bell_draw(splits[4], (SEQ, HEADS * HD), 1.0, 6.0, ((0, 8), (1, 16)))
    log_norm = jnp.clip(4.0 + 2.0 * jax.random.uniform(splits[5], (HEADS, SEQ), jnp.float32) ** level_of(splits[5], (HEADS, SEQ), ((0, 16), (1, 8)), -0.2, 0.2), 4.0, 6.0)
    doc_ids = jnp.searchsorted(jnp.cumsum(uneven(splits[6], N_CTX, SEQ, SEQ // 2 + TOK_DEV, 2)), jnp.arange(SEQ), side="right").astype(jnp.int32)
    return dict(queries=queries, keys=keys, values=values, outputs=outputs, out_grad=out_grad, log_norm=log_norm, doc_ids=doc_ids)


def reference(queries, keys, values, outputs, out_grad, log_norm, doc_ids):
    scale = float(HD) ** -0.5
    places = jnp.arange(SEQ, dtype=jnp.int32)
    allowed = (places[None, :] <= places[:, None]) & (doc_ids[None, :] == doc_ids[:, None])

    def one_head(carry, head):
        key_acc, value_acc = carry
        start = (head * HD).astype(jnp.int32)
        query = lax.dynamic_slice_in_dim(queries, start, HD, 1)
        output = lax.dynamic_slice_in_dim(outputs, start, HD, 1)
        cotan = lax.dynamic_slice_in_dim(out_grad, start, HD, 1)
        lse_row = lax.dynamic_index_in_dim(log_norm, head, 0, keepdims=False)
        scores = jnp.dot(query, keys.T, preferred_element_type=jnp.float32) * scale
        prob = jnp.where(allowed, jnp.exp(scores - lse_row[:, None]), jnp.float32(0.0))
        prob_low = prob.astype(jnp.bfloat16)
        dprob = jnp.dot(cotan, values.T, preferred_element_type=jnp.float32)
        delta = jnp.sum(cotan.astype(jnp.float32) * output.astype(jnp.float32), axis=-1)
        dscore = (prob * (dprob - delta[:, None])).astype(jnp.bfloat16)
        query_part = (jnp.dot(dscore, keys, preferred_element_type=jnp.float32) * scale).astype(jnp.bfloat16)
        key_acc = key_acc + jnp.dot(dscore.T, query, preferred_element_type=jnp.float32) * scale
        value_acc = value_acc + jnp.dot(prob_low.T, cotan, preferred_element_type=jnp.float32)
        return (key_acc, value_acc), query_part

    zeros = jnp.zeros((SEQ, HD), jnp.float32)
    (key_acc, value_acc), parts = lax.scan(one_head, (zeros, zeros), jnp.arange(HEADS, dtype=jnp.int32))
    query_grad = jnp.transpose(parts, (1, 0, 2)).reshape(SEQ, HEADS * HD)
    return query_grad, key_acc.astype(jnp.bfloat16), value_acc.astype(jnp.bfloat16)
```

```python
import functools
import math

import jax
import jax.numpy as jnp
from jax import lax
from jax.experimental import pallas as pl
from jax.experimental.pallas import tpu as pltpu
from jax.sharding import PartitionSpec as P

MESH = pl.DeviceIdType.MESH
SPAN = 5120
FAR = 8192.0
F32 = jnp.float32
BF16 = jnp.bfloat16


def split3(x):
    hi = x.astype(BF16).astype(F32)
    mid = (x - hi).astype(BF16).astype(F32)
    return hi, mid, x - hi - mid


def dot(a, b):
    return jnp.dot(a, b, preferred_element_type=F32)


def kernel(
    n_ctx, n_tp, steps,
    q_in, k_in, v_in, o_in, g_in, lse_in, doc_in,
    dq_out, dk_out, dv_out,
    qn, gn, on, qt, gt, xt, kv, fk, kt, acc, dqt, dqs, part, rs, back, fin, tot,
    lse, doc, doc_a, doc_b,
    in_sem, sib_send, sib_recv, s1, r1, s2, r2, s3, r3, s4, r4,
):
    rows, hd = qn.shape[1], qn.shape[2]
    half = n_tp // 2
    own = rows // n_tp
    width = own * half
    lines = rows // 128
    scale = float(hd) ** -0.5
    c = lax.axis_index("ctx")
    t = lax.axis_index("tp")
    core = t % 2
    u = t // 2
    sib = (c, t + 1 - 2 * core)
    mine = pl.ds(pl.multiple_of(u * own, own), own)

    loads = [
        pltpu.make_async_copy(src, dst, in_sem.at[i])
        for i, (src, dst) in enumerate((
            (k_in, kv.at[0, 0, mine]), (v_in, kv.at[0, 1, mine]), (q_in, qn.at[0]), (g_in, gn.at[0]),
            (o_in, on), (lse_in, lse), (doc_in, doc),
        ))
    ]
    for load in loads:
        load.start()

    barrier = pltpu.get_barrier_semaphore()
    pl.semaphore_signal(barrier, inc=1, device_id=sib, device_id_type=MESH)

    def greet_tp(j, _):
        pl.semaphore_signal(barrier, inc=1, device_id=(c, ((u + j) % half) * 2 + core), device_id_type=MESH)
        return 0

    def greet_ctx(j, _):
        pl.semaphore_signal(barrier, inc=1, device_id=((c + j) % n_ctx, t), device_id_type=MESH)
        return 0

    lax.fori_loop(1, half, greet_tp, 0)
    lax.fori_loop(1, n_ctx, greet_ctx, 0)
    for load in loads[:4]:
        load.wait()
    pl.semaphore_wait(barrier, 1 + half - 1 + n_ctx - 1)

    def copy1(s):
        return pltpu.make_async_remote_copy(
            kv.at[0, :, mine], kv.at[s, :, mine], s1.at[s], r1.at[s], ((c + s) % n_ctx, t), MESH)

    def copy2(s, j):
        return pltpu.make_async_remote_copy(
            kv.at[s, :, mine], kv.at[s, :, mine], s2.at[s], r2.at[s], (c, ((u + j) % half) * 2 + core), MESH)

    def spread(s):
        def one(j, _):
            copy2(s, j).start()
            return 0
        lax.fori_loop(1, half, one, 0)

    def for_steps(first, last, fn):
        def one(s, _):
            fn(s)
            return 0
        lax.fori_loop(first, last, one, 0)

    def when_sends(fn):
        def run(s):
            @pl.when(c + s < n_ctx)
            def _():
                fn(s)
        return run

    def when_has(fn):
        def run(s):
            @pl.when(c >= s)
            def _():
                fn(s)
        return run

    for_steps(1, steps, when_sends(lambda s: copy1(s).start()))
    spread(0)
    sib_q = pltpu.make_async_remote_copy(qn.at[0], qn.at[1], sib_send.at[0], sib_recv.at[0], sib, MESH)
    sib_g = pltpu.make_async_remote_copy(gn.at[0], gn.at[1], sib_send.at[1], sib_recv.at[1], sib, MESH)
    sib_x = pltpu.make_async_remote_copy(
        xt.at[0, pl.ds(0, 16)], xt.at[1, pl.ds(0, 16)], sib_send.at[2], sib_recv.at[2], sib, MESH)
    sib_d = pltpu.make_async_remote_copy(dqt.at[1], dqs, sib_send.at[3], sib_recv.at[3], sib, MESH)
    sib_q.start()
    sib_g.start()

    for load in loads[4:]:
        load.wait()
    g_t = gn[0].T
    qt[0] = qn[0].T
    gt[0] = g_t
    delta = jnp.sum(g_t.astype(F32) * on[...].T.astype(F32), axis=0, keepdims=True)
    q_doc = jnp.concatenate([doc[pl.ds(c * lines + j, 1), :] for j in range(lines)], axis=1)
    place = lax.broadcasted_iota(jnp.int32, (8, rows), 0)
    extra = jnp.zeros((8, rows), F32)
    for i, row in enumerate((*split3(lse[...] * math.sqrt(hd)), *split3(delta))):
        extra = jnp.where(place == i, -row, extra)
    xt[0, 0:8, :] = jnp.where(place == q_doc, -FAR, 0.0).astype(BF16)
    xt[0, 8:16, :] = extra.astype(BF16)
    sib_x.start()
    for h in range(2):
        xt[h, 16:, :] = jnp.zeros((hd - 16, rows), BF16)

    for_steps(1, steps, when_has(lambda s: (copy1(s).wait_recv(), spread(s))))

    turned = pltpu.roll(doc[...], 64, 1)
    doc_a[...] = jnp.where(core == 0, doc[...], turned)
    doc_b[...] = jnp.where(core == 0, turned, doc[...])
    lane = lax.broadcasted_iota(jnp.int32, (128, 128), 1)

    def features(s):
        for m in range(lines // 2):
            at = (c - s) * lines + 2 * m
            both = jnp.where(lane < 64, doc_a[pl.ds(at, 1), :], doc_b[pl.ds(at + 1, 1), :])
            other = jnp.where((lane < 11) & (both.T != lane), 1.0, 0.0)
            fk[s, m * 128:(m + 1) * 128, :] = other.astype(BF16)

    for_steps(0, steps, when_has(features))

    v_lane = lax.broadcasted_iota(jnp.int32, (1, 128), 1)
    v_row = jnp.where((v_lane >= 11) & (v_lane < 14), 1.0, 0.0).astype(BF16)

    def arrive(s):
        got = kv.at[s, :, pl.ds(0, width - own)]
        pltpu.make_async_copy(got, got, r2.at[s]).wait()
        kt[...] = kv[s, 0].T
        acc[...] = jnp.zeros_like(acc)

    def tile(h, s, q0, tq, k0, tk, diagonal):
        qs, ks = pl.ds(q0, tq), pl.ds(k0, tk)
        x = xt[h, :, qs]
        k_all = jnp.concatenate([kv[s, 0, ks], fk[s, ks]], axis=1)
        v_all = jnp.concatenate([kv[s, 1, ks], jnp.broadcast_to(v_row, (tk, 128))], axis=1)
        prob = jnp.exp2(dot(k_all, jnp.concatenate([qt[h, :, qs], x], axis=0)) * (scale * math.log2(math.e)))
        if diagonal:
            r = k0 + lax.broadcasted_iota(jnp.int32, (tk, tq), 0)
            k_pos = (r // own * 2 + core) * own + r % own
            prob = jnp.where(k_pos <= q0 + lax.broadcasted_iota(jnp.int32, (tk, tq), 1), prob, 0.0)
        dprob = dot(v_all, jnp.concatenate([gt[h, :, qs], x], axis=0))
        low = prob.astype(BF16)
        dscore = (prob * dprob).astype(BF16)
        acc[0, ks] += dot(dscore, qn[h, qs])
        acc[1, ks] += dot(low, gn[h, qs])
        dqt[h, :, qs] += dot(kt[:, ks], dscore)

    def copy3(s, j):
        to = (u + j) % half
        rows_to = pl.ds(pl.multiple_of(to * own, own), own)
        return pltpu.make_async_remote_copy(
            part.at[s, :, rows_to], rs.at[s, j - 1], s3.at[s], r3.at[s], (c, to * 2 + core), MESH)

    def hand_out(s):
        part[s] = acc[...].astype(BF16)

        def one(j, _):
            copy3(s, j).start()
            return 0
        lax.fori_loop(1, half, one, 0)

    def gathered(s):
        pltpu.make_async_copy(rs.at[s], rs.at[s], r3.at[s]).wait()
        total = part[s, :, mine].astype(F32)
        for j in range(half - 1):
            total += rs[s, j].astype(F32)
        return total

    def copy4(s):
        return pltpu.make_async_remote_copy(
            back.at[s], fin.at[s], s4.at[s], r4.at[s], ((c + n_ctx - s) % n_ctx, t), MESH)

    def reduce(s):
        back[s] = gathered(s).astype(BF16)
        copy4(s).start()

    dqt[...] = jnp.zeros_like(dqt)
    tq = min(256, rows)

    arrive(0)

    def own_tiles(h):
        for q0 in range(0, rows, tq):
            tile(h, 0, q0, tq, 0, (q0 + tq) // 2, True)

    own_tiles(0)
    sib_q.wait_recv()
    sib_g.wait_recv()
    sib_x.wait_recv()
    qt[1] = qn[1].T
    gt[1] = gn[1].T
    own_tiles(1)
    hand_out(0)
    pl.when(c == 0)(lambda: sib_d.start())

    def step(s):
        def work():
            arrive(s)

            def two(i, _):
                h = 1 - i
                if isinstance(s, int) and s * rows == SPAN:
                    for q0 in range(0, rows, tq):
                        tile(h, s, q0, tq, q0 // 2, width - q0 // 2, False)
                else:
                    def over(n, _):
                        tile(h, s, pl.multiple_of(n * tq, tq), tq, 0, width, False)
                        return 0
                    lax.fori_loop(0, rows // tq, over, 0)

                @pl.when((i == 0) & ((c == s) | (s == steps - 1)))
                def _():
                    sib_d.start()
                return 0

            lax.fori_loop(0, 2, two, 0)
            hand_out(s)

        pl.when(c >= s)(work)

    last = steps - 1 if (steps - 1) * rows == SPAN else steps
    if last > 1:
        step(1)
        tot[...] = gathered(0)

    def middle(s):
        step(s)
        pl.when(c >= s - 1)(lambda: reduce(s - 1))

    for_steps(2, last, middle)
    if last < steps:
        middle(last)
    pl.when(c >= steps - 1)(lambda: reduce(steps - 1))

    sib_d.wait_recv()
    dq_out[...] = ((dqt[0] + dqs[...]) * scale).T.astype(BF16)

    def collect(s):
        copy4(s).wait_recv()
        tot[...] += fin[s].astype(F32)

    for_steps(1, steps, when_sends(collect))
    dk_out[...] = (tot[0] * scale).astype(BF16)
    dv_out[...] = tot[1].astype(BF16)

    sib_q.wait_send()
    sib_g.wait_send()
    sib_x.wait_send()
    sib_d.wait_send()

    def sent(s):
        out = kv.at[s, :, pl.ds(0, width - own)]
        pltpu.make_async_copy(out, out, s2.at[s]).wait()
        gone = part.at[s, :, pl.ds(0, width - own)]
        pltpu.make_async_copy(gone, gone, s3.at[s]).wait()

    for_steps(0, steps, when_has(sent))
    for_steps(1, steps, when_sends(lambda s: copy1(s).wait_send()))
    for_steps(1, steps, when_has(lambda s: copy4(s).wait_send()))


def body(n_ctx, n_tp, queries, keys, values, outputs, out_grad, log_norm, doc_ids):
    rows, hd = queries.shape
    own = keys.shape[0]
    half = n_tp // 2
    width = own * half
    steps = min(n_ctx, -(-SPAN // rows) + 1)
    doc_ids = doc_ids.reshape(-1, 128)
    dma = pltpu.SemaphoreType.DMA
    anywhere = pl.BlockSpec(memory_space=pl.ANY)
    inside = pl.BlockSpec(memory_space=pltpu.VMEM)
    return pl.pallas_call(
        functools.partial(kernel, n_ctx, n_tp, steps),
        out_shape=(
            jax.ShapeDtypeStruct((rows, hd), BF16),
            jax.ShapeDtypeStruct((own, hd), BF16),
            jax.ShapeDtypeStruct((own, hd), BF16),
        ),
        in_specs=[anywhere] * 7,
        out_specs=(inside, inside, inside),
        scratch_shapes=[
            pltpu.VMEM((2, rows, hd), BF16),
            pltpu.VMEM((2, rows, hd), BF16),
            pltpu.VMEM((rows, hd), BF16),
            pltpu.VMEM((2, hd, rows), BF16),
            pltpu.VMEM((2, hd, rows), BF16),
            pltpu.VMEM((2, hd, rows), BF16),
            pltpu.VMEM((steps, 2, width, hd), BF16),
            pltpu.VMEM((steps, width, hd), BF16),
            pltpu.VMEM((hd, width), BF16),
            pltpu.VMEM((2, width, hd), F32),
            pltpu.VMEM((2, hd, rows), F32),
            pltpu.VMEM((hd, rows), F32),
            pltpu.VMEM((steps, 2, width, hd), BF16),
            pltpu.VMEM((steps, half - 1, 2, own, hd), BF16),
            pltpu.VMEM((steps, 2, own, hd), BF16),
            pltpu.VMEM((steps, 2, own, hd), BF16),
            pltpu.VMEM((2, own, hd), F32),
            pltpu.VMEM((1, rows), F32),
            pltpu.VMEM(doc_ids.shape, jnp.int32),
            pltpu.VMEM(doc_ids.shape, jnp.int32),
            pltpu.VMEM(doc_ids.shape, jnp.int32),
            dma((7,)), dma((4,)), dma((4,)),
            *[dma((steps,)) for _ in range(8)],
        ],
        compiler_params=pltpu.CompilerParams(
            collective_id=0, has_side_effects=True, vmem_limit_bytes=48 * 1024 * 1024),
    )(queries, keys, values, outputs, out_grad, log_norm, doc_ids)


def solution(mesh):
    return jax.shard_map(
        functools.partial(body, mesh.shape["ctx"], mesh.shape["tp"]),
        mesh=mesh,
        in_specs=(
            P("ctx", "tp"),
            P(("ctx", "tp"), None),
            P(("ctx", "tp"), None),
            P("ctx", "tp"),
            P("ctx", "tp"),
            P("tp", "ctx"),
            P(),
        ),
        out_specs=(P("ctx", "tp"), P(("ctx", "tp"), None), P(("ctx", "tp"), None)),
        check_vma=False,
    )
```

```python
import functools
import math

import jax
import jax.numpy as jnp
from jax import lax
from jax.experimental import pallas as pl
from jax.experimental.pallas import tpu as pltpu
from jax.sharding import PartitionSpec as P

MESH = pl.DeviceIdType.MESH
SPAN = 5120
FAR = 8192.0
F32 = jnp.float32
BF16 = jnp.bfloat16


def split3(x):
    hi = x.astype(BF16).astype(F32)
    mid = (x - hi).astype(BF16).astype(F32)
    return hi, mid, x - hi - mid


def dot(a, b):
    return jnp.dot(a, b, preferred_element_type=F32)


def kernel(
    n_ctx, n_tp, steps,
    q_in, k_in, v_in, o_in, g_in, lse_in, doc_in,
    dq_out, dk_out, dv_out,
    qn, gn, on, qt, gt, xt, kb, vb, fk, acc, dqt, dqs,
    part_k, rs_k, y_out, y_own, z_in, back, fin_k, tot_k,
    part_v, fin_v, tot_v, out_v, rs_v,
    lse, doc, doc_a, doc_b,
    in_sem, sib_send, sib_recv, near_send, near_recv, last_send, last_recv,
    s_a, r_a, s_z, r_z, s_y, r_y, s_b, r_b, s_p, r_p, s_q, r_q, s_f, r_f, s_g, r_g,
):
    rows, hd = qn.shape[1], qn.shape[2]
    half = n_tp // 2
    ys = half // 2
    own = rows // n_tp
    width = own * half
    lines = rows // 128
    scale = float(hd) ** -0.5
    c = lax.axis_index("ctx")
    t = lax.axis_index("tp")
    core = t % 2
    u = t // 2
    y = u % ys
    z = u // ys
    sib = (c, t + 1 - 2 * core)
    over_z = (c, ((1 - z) * ys + y) * 2 + core)

    loads = [
        pltpu.make_async_copy(src, dst, in_sem.at[i])
        for i, (src, dst) in enumerate((
            (k_in, kb.at[0, z, y]), (v_in, vb.at[0, z, y]), (q_in, qn.at[0]), (g_in, gn.at[0]),
            (o_in, on), (lse_in, lse), (doc_in, doc),
        ))
    ]
    for load in loads:
        load.start()

    def loop(first, last, fn):
        def one(i, _):
            fn(i)
            return 0
        lax.fori_loop(first, last, one, 0)

    def when_sends(fn):
        def run(s):
            @pl.when(c + s < n_ctx)
            def _():
                fn(s)
        return run

    def when_has(fn):
        def run(s):
            @pl.when(c >= s)
            def _():
                fn(s)
        return run

    def remote(src, dst, send, recv, to):
        return pltpu.make_async_remote_copy(src, dst, send, recv, to, MESH)

    def await_bytes(ref, sem):
        pltpu.make_async_copy(ref, ref, sem).wait()

    def peer(j):
        v = (u + j) % half
        return v // ys, v % ys, (c, v * 2 + core)

    def y_peer(j):
        w = (y + j) % ys
        return w, (c, (z * ys + w) * 2 + core)

    barrier = pltpu.get_barrier_semaphore()

    def greet(to):
        pl.semaphore_signal(barrier, inc=1, device_id=to, device_id_type=MESH)

    greet(sib)
    loop(1, half, lambda j: greet(peer(j)[2]))
    loop(1, n_ctx, lambda j: greet(((c + j) % n_ctx, t)))
    for load in loads[:2]:
        load.wait()
    pl.semaphore_wait(barrier, 1 + half - 1 + n_ctx - 1)

    def near_k(j):
        return remote(kb.at[0, z, y], kb.at[0, z, y], near_send.at[0], near_recv.at[0], peer(j)[2])

    def near_v(j):
        return remote(vb.at[0, z, y], vb.at[0, z, y], near_send.at[1], near_recv.at[1], peer(j)[2])

    def along_ctx(s):
        return remote(kb.at[0, z, y], kb.at[s, z, y], s_a.at[s], r_a.at[s], ((c + s) % n_ctx, t))

    def across_z(s):
        return remote(kb.at[s, z, y], kb.at[s, z, y], s_z.at[s], r_z.at[s], over_z)

    def along_y(s, j):
        return remote(kb.at[s, :, y], kb.at[s, :, y], s_y.at[s], r_y.at[s], y_peer(j)[1])

    def block_v(s):
        return remote(vb.at[0], vb.at[s], s_b.at[s], r_b.at[s], ((c + s) % n_ctx, t))

    loop(1, half, lambda j: near_k(j).start())
    loop(1, steps, when_sends(lambda s: along_ctx(s).start()))
    loop(1, half, lambda j: near_v(j).start())
    for load in loads[2:4]:
        load.wait()
    sib_q = remote(qn.at[0], qn.at[1], sib_send.at[0], sib_recv.at[0], sib)
    sib_g = remote(gn.at[0], gn.at[1], sib_send.at[1], sib_recv.at[1], sib)
    sib_x = remote(xt.at[0, pl.ds(0, 16)], xt.at[1, pl.ds(0, 16)], sib_send.at[2], sib_recv.at[2], sib)
    sib_d = remote(dqt.at[1], dqs, sib_send.at[3], sib_recv.at[3], sib)
    sib_q.start()
    sib_g.start()

    for load in loads[4:]:
        load.wait()
    g_t = gn[0].T
    qt[0] = qn[0].T
    gt[0] = g_t
    delta = jnp.sum(g_t.astype(F32) * on[...].T.astype(F32), axis=0, keepdims=True)
    q_doc = jnp.concatenate([doc[pl.ds(c * lines + j, 1), :] for j in range(lines)], axis=1)
    place = lax.broadcasted_iota(jnp.int32, (8, rows), 0)
    extra = jnp.zeros((8, rows), F32)
    for i, row in enumerate((*split3(lse[...] * math.sqrt(hd)), *split3(delta))):
        extra = jnp.where(place == i, -row, extra)
    xt[0, 0:8, :] = jnp.where(place == q_doc, -FAR, 0.0).astype(BF16)
    xt[0, 8:16, :] = extra.astype(BF16)
    sib_x.start()

    loop(1, steps, when_has(lambda s: along_ctx(s).wait_recv()))
    loop(1, steps, when_has(lambda s: across_z(s).start()))

    for h in range(2):
        xt[h, 16:, :] = jnp.zeros((hd - 16, rows), BF16)
    turned = pltpu.roll(doc[...], 64, 1)
    doc_a[...] = jnp.where(core == 0, doc[...], turned)
    doc_b[...] = jnp.where(core == 0, turned, doc[...])
    lane = lax.broadcasted_iota(jnp.int32, (128, 128), 1)

    def features(s):
        for m in range(lines // 2):
            at = (c - s) * lines + 2 * m
            both = jnp.where(lane < 64, doc_a[pl.ds(at, 1), :], doc_b[pl.ds(at + 1, 1), :])
            other = jnp.where((lane < 11) & (both.T != lane), 1.0, 0.0)
            fk[s, m * 128:(m + 1) * 128, :] = other.astype(BF16)

    loop(0, steps, when_has(features))
    dqt[...] = jnp.zeros_like(dqt)

    await_bytes(rs_v, near_recv.at[1])
    loop(1, steps, when_sends(lambda s: block_v(s).start()))
    await_bytes(rs_v, near_recv.at[0])

    def spread_y(s):
        across_z(s).wait_recv()
        loop(1, ys, lambda j: along_y(s, j).start())

    v_lane = lax.broadcasted_iota(jnp.int32, (1, 128), 1)
    v_row = jnp.where((v_lane >= 11) & (v_lane < 14), 1.0, 0.0).astype(BF16)

    def tile(h, s, q0, tq, k0, tk, diagonal):
        qs, ks = pl.ds(q0, tq), pl.ds(k0, tk)
        x = xt[h, :, qs]
        k_own = kb[s].reshape(width, hd)[k0:k0 + tk]
        v_own = vb[s].reshape(width, hd)[k0:k0 + tk]
        k_all = jnp.concatenate([k_own, fk[s, ks]], axis=1)
        v_all = jnp.concatenate([v_own, jnp.broadcast_to(v_row, (tk, 128))], axis=1)
        prob = jnp.exp2(dot(k_all, jnp.concatenate([qt[h, :, qs], x], axis=0)) * (scale * math.log2(math.e)))
        if diagonal:
            r = k0 + lax.broadcasted_iota(jnp.int32, (tk, tq), 0)
            k_pos = (r // own * 2 + core) * own + r % own
            prob = jnp.where(k_pos <= q0 + lax.broadcasted_iota(jnp.int32, (tk, tq), 1), prob, 0.0)
        dprob = dot(v_all, jnp.concatenate([gt[h, :, qs], x], axis=0))
        low = prob.astype(BF16)
        dscore = (prob * dprob).astype(BF16)
        acc[0, ks] += dot(dscore, qn[h, qs])
        acc[1, ks] += dot(low, gn[h, qs])
        dqt[h, :, qs] += dot(k_own.T, dscore)

    def to_y(s, j):
        w, to = y_peer(j)
        return remote(part_k.at[s, :, w], rs_k.at[s, j - 1], s_p.at[s], r_p.at[s], to)

    def to_z(s):
        return remote(y_out.at[s], z_in.at[s], s_q.at[s], r_q.at[s], over_z)

    def to_owner(s):
        return remote(back.at[s], fin_k.at[s], s_f.at[s], r_f.at[s], ((c + n_ctx - s) % n_ctx, t))

    def v_to_owner(s):
        return remote(part_v.at[s], fin_v.at[s], s_g.at[s], r_g.at[s], ((c + n_ctx - s) % n_ctx, t))

    def hand_out(s):
        part_k[s] = acc[0].astype(BF16).reshape(2, ys, own, hd)
        loop(1, ys, lambda j: to_y(s, j).start())
        if isinstance(s, int) and s == 0:
            tot_v[...] = acc[1]
        else:
            part_v[s] = acc[1].astype(BF16)
            v_to_owner(s).start()

    def sum_y(s):
        await_bytes(rs_k.at[s], r_p.at[s])

        def total(at):
            full = part_k[s, at, y].astype(F32)
            for j in range(ys - 1):
                full += rs_k[s, j, at].astype(F32)
            return full
        y_own[s] = total(z)
        y_out[s] = total(1 - z).astype(BF16)
        to_z(s).start()

    def sum_z(s):
        to_z(s).wait_recv()
        full = y_own[s] + z_in[s].astype(F32)
        if isinstance(s, int) and s == 0:
            tot_k[...] = full
        else:
            back[s] = full.astype(BF16)
            to_owner(s).start()

    tq = min(256, rows)

    def edge(h, s):
        for q0 in range(0, rows, tq):
            if s == 0:
                tile(h, s, q0, tq, 0, (q0 + tq) // 2, True)
            else:
                tile(h, s, q0, tq, q0 // 2, width - q0 // 2, False)

    acc[...] = jnp.zeros_like(acc)
    edge(0, 0)
    loop(1, steps, when_has(spread_y))
    sib_q.wait_recv()
    sib_g.wait_recv()
    sib_x.wait_recv()
    qt[1] = qn[1].T
    gt[1] = gn[1].T
    edge(1, 0)
    hand_out(0)
    pl.when(c == 0)(lambda: sib_d.start())

    last = steps - 1 if (steps - 1) * rows == SPAN else steps

    def step(s):
        edged = isinstance(s, int) and s == last
        before = s - 1

        @pl.when(c >= s)
        def _():
            await_bytes(part_k.at[s, :, pl.ds(0, ys - 1)], r_y.at[s])
            block_v(s).wait_recv()
            acc[...] = jnp.zeros_like(acc)
            for h in (1, 0):
                if edged:
                    edge(h, s)
                else:
                    tile(h, s, 0, rows, 0, width, False)
                if h == 1:
                    @pl.when((c == s) | (s == steps - 1))
                    def _():
                        sib_d.start()
                    sum_y(before)
            hand_out(s)

        @pl.when(c == before)
        def _():
            sum_y(before)

        @pl.when(c >= before)
        def _():
            sum_z(before)

    if steps > 1:
        step(1)
    loop(2, last, step)
    if 1 < last < steps:
        step(last)

    @pl.when(c >= steps - 1)
    def _():
        sum_y(steps - 1)
        sum_z(steps - 1)

    sib_d.wait_recv()
    dq_out[...] = ((dqt[0] + dqs[...]) * scale).T.astype(BF16)

    def collect_v(s):
        v_to_owner(s).wait_recv()
        tot_v[...] += fin_v[s].astype(F32).reshape(width, hd)

    def collect_k(s):
        to_owner(s).wait_recv()
        tot_k[...] += fin_k[s].astype(F32)

    def last_v(j):
        pz, py, to = peer(j)
        return remote(out_v.at[pz, py], rs_v.at[j - 1], last_send, last_recv, to)

    loop(1, steps, when_sends(collect_v))
    out_v[...] = tot_v[...].astype(BF16).reshape(2, ys, own, hd)
    loop(1, half, lambda j: last_v(j).start())
    loop(1, steps, when_sends(collect_k))
    dk_out[...] = (tot_k[...] * scale).astype(BF16)
    await_bytes(rs_v, last_recv)
    full = out_v[z, y].astype(F32)
    for j in range(half - 1):
        full += rs_v[j].astype(F32)
    dv_out[...] = full.astype(BF16)

    for copy in (sib_q, sib_g, sib_x, sib_d):
        copy.wait_send()
    await_bytes(rs_v, near_send.at[0])
    await_bytes(rs_v, near_send.at[1])
    await_bytes(rs_v, last_send)

    def sent_down(s):
        along_ctx(s).wait_send()
        block_v(s).wait_send()

    def sent_up(s):
        across_z(s).wait_send()
        await_bytes(rs_k.at[s], s_y.at[s])
        to_owner(s).wait_send()
        v_to_owner(s).wait_send()

    def sent_sums(s):
        await_bytes(rs_k.at[s], s_p.at[s])
        to_z(s).wait_send()

    loop(1, steps, when_sends(sent_down))
    loop(1, steps, when_has(sent_up))
    loop(0, steps, when_has(sent_sums))


def body(n_ctx, n_tp, queries, keys, values, outputs, out_grad, log_norm, doc_ids):
    rows, hd = queries.shape
    own = keys.shape[0]
    half = n_tp // 2
    width = own * half
    steps = min(n_ctx, -(-SPAN // rows) + 1)
    doc_ids = doc_ids.reshape(-1, 128)
    dma = pltpu.SemaphoreType.DMA
    anywhere = pl.BlockSpec(memory_space=pl.ANY)
    inside = pl.BlockSpec(memory_space=pltpu.VMEM)
    return pl.pallas_call(
        functools.partial(kernel, n_ctx, n_tp, steps),
        out_shape=(
            jax.ShapeDtypeStruct((rows, hd), BF16),
            jax.ShapeDtypeStruct((own, hd), BF16),
            jax.ShapeDtypeStruct((own, hd), BF16),
        ),
        in_specs=[anywhere] * 7,
        out_specs=(inside, inside, inside),
        scratch_shapes=[
            pltpu.VMEM((2, rows, hd), BF16),
            pltpu.VMEM((2, rows, hd), BF16),
            pltpu.VMEM((rows, hd), BF16),
            pltpu.VMEM((2, hd, rows), BF16),
            pltpu.VMEM((2, hd, rows), BF16),
            pltpu.VMEM((2, hd, rows), BF16),
            pltpu.VMEM((steps, 2, half // 2, own, hd), BF16),
            pltpu.VMEM((steps, 2, half // 2, own, hd), BF16),
            pltpu.VMEM((steps, width, hd), BF16),
            pltpu.VMEM((2, width, hd), F32),
            pltpu.VMEM((2, hd, rows), F32),
            pltpu.VMEM((hd, rows), F32),
            pltpu.VMEM((steps, 2, half // 2, own, hd), BF16),
            pltpu.VMEM((steps, half // 2 - 1, 2, own, hd), BF16),
            pltpu.VMEM((steps, own, hd), BF16),
            pltpu.VMEM((steps, own, hd), F32),
            pltpu.VMEM((steps, own, hd), BF16),
            pltpu.VMEM((steps, own, hd), BF16),
            pltpu.VMEM((steps, own, hd), BF16),
            pltpu.VMEM((own, hd), F32),
            pltpu.VMEM((steps, width, hd), BF16),
            pltpu.VMEM((steps, width, hd), BF16),
            pltpu.VMEM((width, hd), F32),
            pltpu.VMEM((2, half // 2, own, hd), BF16),
            pltpu.VMEM((half - 1, own, hd), BF16),
            pltpu.VMEM((1, rows), F32),
            pltpu.VMEM(doc_ids.shape, jnp.int32),
            pltpu.VMEM(doc_ids.shape, jnp.int32),
            pltpu.VMEM(doc_ids.shape, jnp.int32),
            dma((7,)), dma((4,)), dma((4,)), dma((2,)), dma((2,)), dma, dma,
            *[dma((steps,)) for _ in range(16)],
        ],
        compiler_params=pltpu.CompilerParams(
            collective_id=0, has_side_effects=True, vmem_limit_bytes=63 * 1024 * 1024),
    )(queries, keys, values, outputs, out_grad, log_norm, doc_ids)


def solution(mesh):
    return jax.shard_map(
        functools.partial(body, mesh.shape["ctx"], mesh.shape["tp"]),
        mesh=mesh,
        in_specs=(
            P("ctx", "tp"),
            P(("ctx", "tp"), None),
            P(("ctx", "tp"), None),
            P("ctx", "tp"),
            P("ctx", "tp"),
            P("tp", "ctx"),
            P(),
        ),
        out_specs=(P("ctx", "tp"), P(("ctx", "tp"), None), P(("ctx", "tp"), None)),
        check_vma=False,
    )
```

```python
import functools
import math

import jax
import jax.numpy as jnp
from jax import lax
from jax.experimental import pallas as pl
from jax.experimental.pallas import tpu as pltpu
from jax.sharding import PartitionSpec as P

MESH = pl.DeviceIdType.MESH
SPAN = 5120
FAR = 8192.0
F32 = jnp.float32
BF16 = jnp.bfloat16


def split3(x):
    hi = x.astype(BF16).astype(F32)
    mid = (x - hi).astype(BF16).astype(F32)
    return hi, mid, x - hi - mid


def dot(a, b):
    return jnp.dot(a, b, preferred_element_type=F32)


def kernel(
    n_ctx, n_tp, steps,
    q_in, k_in, v_in, o_in, g_in, lse_in, doc_in,
    dq_out, dk_out, dv_out,
    qn, gn, on, qt, gt, xt, kb, vb, fk, acc, dqt, dqs,
    part_k, rs_k, y_out, y_own, z_in, back, fin_k, tot_k,
    part_v, fin_v, acc_own, out_k, out_v, own_k, rs_v,
    lse, doc, doc_a, doc_b,
    in_sem, sib_send, sib_recv, near_send, near_recv, last_send, last_recv,
    s_a, r_a, s_z, r_z, s_y, r_y, s_b, r_b, s_p, r_p, s_q, r_q, s_f, r_f, s_g, r_g,
):
    rows, hd = qn.shape[1], qn.shape[2]
    half = n_tp // 2
    ys = half // 2
    own = rows // n_tp
    width = own * half
    lines = rows // 128
    scale = float(hd) ** -0.5
    c = lax.axis_index("ctx")
    t = lax.axis_index("tp")
    core = t % 2
    u = t // 2
    y = u % ys
    z = u // ys
    sib = (c, t + 1 - 2 * core)
    over_z = (c, ((1 - z) * ys + y) * 2 + core)

    loads = [
        pltpu.make_async_copy(src, dst, in_sem.at[i])
        for i, (src, dst) in enumerate((
            (k_in, kb.at[0, z, y]), (v_in, vb.at[0, z, y]), (q_in, qn.at[0]), (g_in, gn.at[0]),
            (o_in, on), (lse_in, lse), (doc_in, doc),
        ))
    ]
    for load in loads:
        load.start()

    def loop(first, last, fn):
        def one(i, _):
            fn(i)
            return 0
        lax.fori_loop(first, last, one, 0)

    def down(fn):
        loop(0, steps - 1, lambda i: fn(steps - 1 - i))

    def when_sends(fn):
        def run(s):
            @pl.when(c + s < n_ctx)
            def _():
                fn(s)
        return run

    def when_has(fn):
        def run(s):
            @pl.when(c >= s)
            def _():
                fn(s)
        return run

    def remote(src, dst, send, recv, to):
        return pltpu.make_async_remote_copy(src, dst, send, recv, to, MESH)

    def await_bytes(ref, sem):
        pltpu.make_async_copy(ref, ref, sem).wait()

    def peer(j):
        v = (u + j) % half
        return v // ys, v % ys, (c, v * 2 + core)

    def y_peer(j):
        w = (y + j) % ys
        return w, (c, (z * ys + w) * 2 + core)

    barrier = pltpu.get_barrier_semaphore()

    def greet(to):
        pl.semaphore_signal(barrier, inc=1, device_id=to, device_id_type=MESH)

    greet(sib)
    loop(1, half, lambda j: greet(peer(j)[2]))
    loop(1, n_ctx, lambda j: greet(((c + j) % n_ctx, t)))

    def near_k(j):
        return remote(kb.at[0, z, y], kb.at[0, z, y], near_send.at[0], near_recv.at[0], peer(j)[2])

    def near_v(j):
        return remote(vb.at[0, z, y], vb.at[0, z, y], near_send.at[1], near_recv.at[1], peer(j)[2])

    def along_ctx(s):
        return remote(kb.at[0, z, y], kb.at[s, z, y], s_a.at[s], r_a.at[s], ((c + s) % n_ctx, t))

    def across_z(s):
        return remote(kb.at[s, z, y], kb.at[s, z, y], s_z.at[s], r_z.at[s], over_z)

    def along_y(s, j):
        return remote(kb.at[s, :, y], kb.at[s, :, y], s_y.at[s], r_y.at[s], y_peer(j)[1])

    def block_v(s):
        return remote(vb.at[0], vb.at[s], s_b.at[s], r_b.at[s], ((c + s) % n_ctx, t))

    sib_q = remote(qn.at[0], qn.at[1], sib_send.at[0], sib_recv.at[0], sib)
    sib_g = remote(gn.at[0], gn.at[1], sib_send.at[1], sib_recv.at[1], sib)
    sib_x = remote(xt.at[0, pl.ds(0, 16)], xt.at[1, pl.ds(0, 16)], sib_send.at[2], sib_recv.at[2], sib)
    sib_d = remote(dqt.at[1], dqs, sib_send.at[3], sib_recv.at[3], sib)

    for load in loads:
        load.wait()
    q_doc = jnp.concatenate([doc[pl.ds(c * lines + j, 1), :] for j in range(lines)], axis=1)
    delta = jnp.sum(gn[0].T.astype(F32) * on[...].T.astype(F32), axis=0, keepdims=True)
    place = lax.broadcasted_iota(jnp.int32, (8, rows), 0)
    extra = jnp.zeros((8, rows), F32)
    for i, row in enumerate((*split3(lse[...] * math.sqrt(hd)), *split3(delta))):
        extra = jnp.where(place == i, -row, extra)
    xt[0, 0:8, :] = jnp.where(place == q_doc, -FAR, 0.0).astype(BF16)
    xt[0, 8:16, :] = extra.astype(BF16)

    pl.semaphore_wait(barrier, 1 + half - 1 + n_ctx - 1)
    down(when_sends(lambda s: along_ctx(s).start()))
    loop(1, half, lambda j: near_v(j).start())
    loop(1, half, lambda j: near_k(j).start())
    sib_x.start()
    sib_q.start()
    sib_g.start()

    qt[0] = qn[0].T
    gt[0] = gn[0].T
    for h in range(2):
        xt[h, 16:, :] = jnp.zeros((hd - 16, rows), BF16)
    dqt[...] = jnp.zeros_like(dqt)
    turned = pltpu.roll(doc[...], 64, 1)
    doc_a[...] = jnp.where(core == 0, doc[...], turned)
    doc_b[...] = jnp.where(core == 0, turned, doc[...])
    lane = lax.broadcasted_iota(jnp.int32, (128, 128), 1)

    def features(s):
        for m in range(lines // 2):
            at = (c - s) * lines + 2 * m
            both = jnp.where(lane < 64, doc_a[pl.ds(at, 1), :], doc_b[pl.ds(at + 1, 1), :])
            other = jnp.where((lane < 11) & (both.T != lane), 1.0, 0.0)
            fk[s, m * 128:(m + 1) * 128, :] = other.astype(BF16)

    features(0)
    down(when_has(lambda s: along_ctx(s).wait_recv()))
    down(when_has(lambda s: across_z(s).start()))
    sib_x.wait_recv()
    sib_q.wait_recv()
    sib_g.wait_recv()
    qt[1] = qn[1].T
    gt[1] = gn[1].T

    await_bytes(rs_v, near_recv.at[1])
    down(when_sends(lambda s: block_v(s).start()))
    await_bytes(rs_v, near_recv.at[0])

    def spread_y(s):
        across_z(s).wait_recv()
        loop(1, ys, lambda j: along_y(s, j).start())

    down(when_has(spread_y))

    v_lane = lax.broadcasted_iota(jnp.int32, (1, 128), 1)
    v_row = jnp.where((v_lane >= 11) & (v_lane < 14), 1.0, 0.0).astype(BF16)

    def tile(h, s, q0, tq, k0, tk, diagonal, sums):
        qs, ks = pl.ds(q0, tq), pl.ds(k0, tk)
        x = xt[h, :, qs]
        k_own = kb[s].reshape(width, hd)[k0:k0 + tk]
        v_own = vb[s].reshape(width, hd)[k0:k0 + tk]
        k_all = jnp.concatenate([k_own, fk[s, ks]], axis=1)
        v_all = jnp.concatenate([v_own, jnp.broadcast_to(v_row, (tk, 128))], axis=1)
        prob = jnp.exp2(dot(k_all, jnp.concatenate([qt[h, :, qs], x], axis=0)) * (scale * math.log2(math.e)))
        if diagonal:
            r = k0 + lax.broadcasted_iota(jnp.int32, (tk, tq), 0)
            k_pos = (r // own * 2 + core) * own + r % own
            prob = jnp.where(k_pos <= q0 + lax.broadcasted_iota(jnp.int32, (tk, tq), 1), prob, 0.0)
        dprob = dot(v_all, jnp.concatenate([gt[h, :, qs], x], axis=0))
        low = prob.astype(BF16)
        dscore = (prob * dprob).astype(BF16)
        sums[0, ks] += dot(dscore, qn[h, qs])
        sums[1, ks] += dot(low, gn[h, qs])
        dqt[h, :, qs] += dot(k_own.T, dscore)

    def to_y(s, j):
        w, to = y_peer(j)
        return remote(part_k.at[s, :, w], rs_k.at[s, j - 1], s_p.at[s], r_p.at[s], to)

    def to_z(s):
        return remote(y_out.at[s], z_in.at[s], s_q.at[s], r_q.at[s], over_z)

    def to_owner(s):
        return remote(back.at[s], fin_k.at[s], s_f.at[s], r_f.at[s], ((c + n_ctx - s) % n_ctx, t))

    def v_to_owner(s):
        return remote(part_v.at[s], fin_v.at[s], s_g.at[s], r_g.at[s], ((c + n_ctx - s) % n_ctx, t))

    def hand_out(s):
        part_k[s] = acc[0].astype(BF16).reshape(2, ys, own, hd)
        loop(1, ys, lambda j: to_y(s, j).start())
        part_v[s] = acc[1].astype(BF16)
        v_to_owner(s).start()

    def sum_y(s):
        await_bytes(rs_k.at[s], r_p.at[s])

        def total(at):
            full = part_k[s, at, y].astype(F32)
            for j in range(ys - 1):
                full += rs_k[s, j, at].astype(F32)
            return full
        y_own[s] = total(z)
        y_out[s] = total(1 - z).astype(BF16)
        to_z(s).start()

    def sum_z(s):
        to_z(s).wait_recv()
        back[s] = (y_own[s] + z_in[s].astype(F32)).astype(BF16)
        to_owner(s).start()

    tq = min(256, rows)

    def edge(h, s, sums):
        for q0 in range(0, rows, tq):
            if s == 0:
                tile(h, s, q0, tq, 0, (q0 + tq) // 2, True, sums)
            else:
                tile(h, s, q0, tq, q0 // 2, width - q0 // 2, False, sums)

    acc_own[...] = jnp.zeros_like(acc_own)
    edge(1, 0, acc_own)
    pl.when(c == 0)(lambda: sib_d.start())
    down(when_has(features))

    def once(s, fn):
        if isinstance(s, int) and s >= steps:
            return

        @pl.when((c >= s) & (s < steps))
        def _():
            fn(s)

    def step(s, edged):
        @pl.when(c >= s)
        def _():
            await_bytes(part_k.at[s, :, pl.ds(0, ys - 1)], r_y.at[s])
            block_v(s).wait_recv()
            acc[...] = jnp.zeros_like(acc)
            if edged:
                edge(1, s, acc)
            else:
                tile(1, s, 0, rows, 0, width, False, acc)
            if not isinstance(s, int) or s == 1:
                @pl.when(s == 1)
                def _():
                    sib_d.start()

        once(s + 2, sum_y)
        once(s + 3, sum_z)

        @pl.when(c >= s)
        def _():
            if edged:
                edge(0, s, acc)
            else:
                tile(0, s, 0, rows, 0, width, False, acc)
            hand_out(s)

    first = steps - 1
    if first * rows == SPAN:
        step(first, True)
        first -= 1
    loop(0, first, lambda i: step(first - i, False))

    if steps > 2:
        once(2, sum_y)
    edge(0, 0, acc_own)
    out_k[...] = acc_own[0].astype(BF16).reshape(2, ys, own, hd)

    def last_k(j):
        pz, py, to = peer(j)
        return remote(out_k.at[pz, py], own_k.at[j - 1], last_send.at[0], last_recv.at[0], to)

    def last_v(j):
        pz, py, to = peer(j)
        return remote(out_v.at[pz, py], rs_v.at[j - 1], last_send.at[1], last_recv.at[1], to)

    def collect_v(s):
        v_to_owner(s).wait_recv()
        acc_own[1] += fin_v[s].astype(F32)

    loop(1, half, lambda j: last_k(j).start())
    once(3, sum_z)
    once(1, sum_y)
    once(2, sum_z)
    once(1, sum_z)
    down(when_sends(collect_v))
    out_v[...] = acc_own[1].astype(BF16).reshape(2, ys, own, hd)
    loop(1, half, lambda j: last_v(j).start())

    sib_d.wait_recv()
    dq_out[...] = ((dqt[0] + dqs[...]) * scale).T.astype(BF16)

    await_bytes(rs_v, last_recv.at[0])
    full = out_k[z, y].astype(F32)
    for j in range(half - 1):
        full += own_k[j].astype(F32)
    tot_k[...] = full

    def collect_k(s):
        to_owner(s).wait_recv()
        tot_k[...] += fin_k[s].astype(F32)

    down(when_sends(collect_k))
    dk_out[...] = (tot_k[...] * scale).astype(BF16)
    await_bytes(rs_v, last_recv.at[1])
    full = out_v[z, y].astype(F32)
    for j in range(half - 1):
        full += rs_v[j].astype(F32)
    dv_out[...] = full.astype(BF16)

    for copy in (sib_q, sib_g, sib_x, sib_d):
        copy.wait_send()
    for i in range(2):
        await_bytes(rs_v, near_send.at[i])
        await_bytes(rs_v, last_send.at[i])

    def sent_down(s):
        along_ctx(s).wait_send()
        block_v(s).wait_send()

    def sent_up(s):
        across_z(s).wait_send()
        await_bytes(rs_k.at[s], s_y.at[s])
        to_owner(s).wait_send()
        v_to_owner(s).wait_send()
        await_bytes(rs_k.at[s], s_p.at[s])
        to_z(s).wait_send()

    down(when_sends(sent_down))
    down(when_has(sent_up))


def body(n_ctx, n_tp, queries, keys, values, outputs, out_grad, log_norm, doc_ids):
    rows, hd = queries.shape
    own = keys.shape[0]
    half = n_tp // 2
    width = own * half
    steps = min(n_ctx, -(-SPAN // rows) + 1)
    doc_ids = doc_ids.reshape(-1, 128)
    dma = pltpu.SemaphoreType.DMA
    anywhere = pl.BlockSpec(memory_space=pl.ANY)
    inside = pl.BlockSpec(memory_space=pltpu.VMEM)
    return pl.pallas_call(
        functools.partial(kernel, n_ctx, n_tp, steps),
        out_shape=(
            jax.ShapeDtypeStruct((rows, hd), BF16),
            jax.ShapeDtypeStruct((own, hd), BF16),
            jax.ShapeDtypeStruct((own, hd), BF16),
        ),
        in_specs=[anywhere] * 7,
        out_specs=(inside, inside, inside),
        scratch_shapes=[
            pltpu.VMEM((2, rows, hd), BF16),
            pltpu.VMEM((2, rows, hd), BF16),
            pltpu.VMEM((rows, hd), BF16),
            pltpu.VMEM((2, hd, rows), BF16),
            pltpu.VMEM((2, hd, rows), BF16),
            pltpu.VMEM((2, hd, rows), BF16),
            pltpu.VMEM((steps, 2, half // 2, own, hd), BF16),
            pltpu.VMEM((steps, 2, half // 2, own, hd), BF16),
            pltpu.VMEM((steps, width, hd), BF16),
            pltpu.VMEM((2, width, hd), F32),
            pltpu.VMEM((2, hd, rows), F32),
            pltpu.VMEM((hd, rows), F32),
            pltpu.VMEM((steps, 2, half // 2, own, hd), BF16),
            pltpu.VMEM((steps, half // 2 - 1, 2, own, hd), BF16),
            pltpu.VMEM((steps, own, hd), BF16),
            pltpu.VMEM((steps, own, hd), F32),
            pltpu.VMEM((steps, own, hd), BF16),
            pltpu.VMEM((steps, own, hd), BF16),
            pltpu.VMEM((steps, own, hd), BF16),
            pltpu.VMEM((own, hd), F32),
            pltpu.VMEM((steps, width, hd), BF16),
            pltpu.VMEM((steps, width, hd), BF16),
            pltpu.VMEM((2, width, hd), F32),
            pltpu.VMEM((2, half // 2, own, hd), BF16),
            pltpu.VMEM((2, half // 2, own, hd), BF16),
            pltpu.VMEM((half - 1, own, hd), BF16),
            pltpu.VMEM((half - 1, own, hd), BF16),
            pltpu.VMEM((1, rows), F32),
            pltpu.VMEM(doc_ids.shape, jnp.int32),
            pltpu.VMEM(doc_ids.shape, jnp.int32),
            pltpu.VMEM(doc_ids.shape, jnp.int32),
            dma((7,)), dma((4,)), dma((4,)), dma((2,)), dma((2,)), dma((2,)), dma((2,)),
            *[dma((steps,)) for _ in range(16)],
        ],
        compiler_params=pltpu.CompilerParams(
            collective_id=0, has_side_effects=True, vmem_limit_bytes=63 * 1024 * 1024),
    )(queries, keys, values, outputs, out_grad, log_norm, doc_ids)


def solution(mesh):
    return jax.shard_map(
        functools.partial(body, mesh.shape["ctx"], mesh.shape["tp"]),
        mesh=mesh,
        in_specs=(
            P("ctx", "tp"),
            P(("ctx", "tp"), None),
            P(("ctx", "tp"), None),
            P("ctx", "tp"),
            P("ctx", "tp"),
            P("tp", "ctx"),
            P(),
        ),
        out_specs=(P("ctx", "tp"), P(("ctx", "tp"), None), P(("ctx", "tp"), None)),
        check_vma=False,
    )
```

```python
import functools
import math

import jax
import jax.numpy as jnp
from jax import lax
from jax.experimental import pallas as pl
from jax.experimental.pallas import tpu as pltpu
from jax.sharding import PartitionSpec as P

MESH = pl.DeviceIdType.MESH
SPAN = 5120
FAR = 8192.0
F32 = jnp.float32
BF16 = jnp.bfloat16


def split3(x):
    hi = x.astype(BF16).astype(F32)
    mid = (x - hi).astype(BF16).astype(F32)
    return hi, mid, x - hi - mid


def dot(a, b):
    return jnp.dot(a, b, preferred_element_type=F32)


def kernel(
    n_ctx, n_tp, steps,
    q_in, k_in, v_in, o_in, g_in, lse_in, doc_in,
    dq_out, dk_out, dv_out,
    qn, gn, on, qt, gt, xt, kb, vb, fk, acc, dqt, dqs,
    part_k, rs_k, y_out, y_own, z_in, back, fin_k, tot_k,
    part_v, fin_v, acc_own, out_k, out_v, own_k, rs_v, one_k, one_v, sum_v, tot,
    lse, doc, doc_a, doc_b,
    in_sem, sib_send, sib_recv, near_send, near_recv, last_send, last_recv, one_send, one_recv,
    s_a, r_a, s_z, r_z, s_y, r_y, s_b, r_b, s_p, r_p, s_q, r_q, s_f, r_f, s_g, r_g,
):
    rows, hd = qn.shape[1], qn.shape[2]
    half = n_tp // 2
    ys = half // 2
    own = rows // n_tp
    width = own * half
    lines = rows // 128
    scale = float(hd) ** -0.5
    c = lax.axis_index("ctx")
    t = lax.axis_index("tp")
    core = t % 2
    u = t // 2
    y = u % ys
    z = u // ys
    sib = (c, t + 1 - 2 * core)
    over_z = (c, ((1 - z) * ys + y) * 2 + core)

    loads = [
        pltpu.make_async_copy(src, dst, in_sem.at[i])
        for i, (src, dst) in enumerate((
            (k_in, kb.at[0, z, y]), (v_in, vb.at[0, z, y]), (q_in, qn.at[0]), (g_in, gn.at[0]),
            (o_in, on), (lse_in, lse), (doc_in, doc),
        ))
    ]
    for load in loads:
        load.start()

    def loop(first, last, fn):
        def one(i, _):
            fn(i)
            return 0
        lax.fori_loop(first, last, one, 0)

    def down(fn):
        loop(0, steps - 1, lambda i: fn(steps - 1 - i))

    def when_sends(fn):
        def run(s):
            @pl.when(c + s < n_ctx)
            def _():
                fn(s)
        return run

    def when_has(fn):
        def run(s):
            @pl.when(c >= s)
            def _():
                fn(s)
        return run

    def remote(src, dst, send, recv, to):
        return pltpu.make_async_remote_copy(src, dst, send, recv, to, MESH)

    def await_bytes(ref, sem):
        pltpu.make_async_copy(ref, ref, sem).wait()

    def peer(j):
        v = (u + j) % half
        return v // ys, v % ys, (c, v * 2 + core)

    def y_peer(j):
        w = (y + j) % ys
        return w, (c, (z * ys + w) * 2 + core)

    barrier = pltpu.get_barrier_semaphore()

    def greet(to):
        pl.semaphore_signal(barrier, inc=1, device_id=to, device_id_type=MESH)

    greet(sib)
    loop(1, half, lambda j: greet(peer(j)[2]))
    loop(1, n_ctx, lambda j: greet(((c + j) % n_ctx, t)))

    def near_k(j):
        return remote(kb.at[0, z, y], kb.at[0, z, y], near_send.at[0], near_recv.at[0], peer(j)[2])

    def near_v(j):
        return remote(vb.at[0, z, y], vb.at[0, z, y], near_send.at[1], near_recv.at[1], peer(j)[2])

    def along_ctx(s):
        return remote(kb.at[0, z, y], kb.at[s, z, y], s_a.at[s], r_a.at[s], ((c + s) % n_ctx, t))

    def across_z(s):
        return remote(kb.at[s, z, y], kb.at[s, z, y], s_z.at[s], r_z.at[s], over_z)

    def along_y(s, j):
        return remote(kb.at[s, :, y], kb.at[s, :, y], s_y.at[s], r_y.at[s], y_peer(j)[1])

    def block_v(s):
        return remote(vb.at[0], vb.at[s], s_b.at[s], r_b.at[s], ((c + s) % n_ctx, t))

    sib_q = remote(qn.at[0], qn.at[1], sib_send.at[0], sib_recv.at[0], sib)
    sib_g = remote(gn.at[0], gn.at[1], sib_send.at[1], sib_recv.at[1], sib)
    sib_x = remote(xt.at[0, pl.ds(0, 16)], xt.at[1, pl.ds(0, 16)], sib_send.at[2], sib_recv.at[2], sib)
    sib_d = remote(dqt.at[1], dqs, sib_send.at[3], sib_recv.at[3], sib)

    for load in loads[:2]:
        load.wait()
    pl.semaphore_wait(barrier, 1 + half - 1 + n_ctx - 1)
    down(when_sends(lambda s: along_ctx(s).start()))
    loop(1, half, lambda j: near_v(j).start())
    for load in loads[2:4]:
        load.wait()
    sib_q.start()
    sib_g.start()
    loop(1, half, lambda j: near_k(j).start())
    for load in loads[4:]:
        load.wait()
    q_doc = jnp.concatenate([doc[pl.ds(c * lines + j, 1), :] for j in range(lines)], axis=1)
    delta = jnp.sum(gn[0].T.astype(F32) * on[...].T.astype(F32), axis=0, keepdims=True)
    place = lax.broadcasted_iota(jnp.int32, (8, rows), 0)
    extra = jnp.zeros((8, rows), F32)
    for i, row in enumerate((*split3(lse[...] * math.sqrt(hd)), *split3(delta))):
        extra = jnp.where(place == i, -row, extra)
    xt[0, 0:8, :] = jnp.where(place == q_doc, -FAR, 0.0).astype(BF16)
    xt[0, 8:16, :] = extra.astype(BF16)

    sib_x.start()

    qt[0] = qn[0].T
    gt[0] = gn[0].T
    for h in range(2):
        xt[h, 16:, :] = jnp.zeros((hd - 16, rows), BF16)
    dqt[...] = jnp.zeros_like(dqt)
    turned = pltpu.roll(doc[...], 64, 1)
    doc_a[...] = jnp.where(core == 0, doc[...], turned)
    doc_b[...] = jnp.where(core == 0, turned, doc[...])
    lane = lax.broadcasted_iota(jnp.int32, (128, 128), 1)

    def features(s):
        for m in range(lines // 2):
            at = (c - s) * lines + 2 * m
            both = jnp.where(lane < 64, doc_a[pl.ds(at, 1), :], doc_b[pl.ds(at + 1, 1), :])
            other = jnp.where((lane < 11) & (both.T != lane), 1.0, 0.0)
            fk[s, m * 128:(m + 1) * 128, :] = other.astype(BF16)

    features(0)
    down(when_has(lambda s: along_ctx(s).wait_recv()))
    down(when_has(lambda s: across_z(s).start()))
    sib_x.wait_recv()
    sib_q.wait_recv()
    sib_g.wait_recv()
    qt[1] = qn[1].T
    gt[1] = gn[1].T

    await_bytes(rs_v, near_recv.at[1])

    def spread_y(s):
        across_z(s).wait_recv()
        loop(1, ys, lambda j: along_y(s, j).start())

    ahead = 2

    def wave_v(s):
        @pl.when((c + s + ahead < n_ctx) & (s + ahead < steps))
        def _():
            block_v(s + ahead).wait_send()
        block_v(s).start()

    lead = max(steps - 1 - ahead, 0)
    loop(0, steps - 1 - lead, lambda i: when_sends(wave_v)(steps - 1 - i))
    loop(0, steps - 1 - lead, lambda i: when_has(spread_y)(steps - 1 - i))
    await_bytes(rs_v, near_recv.at[0])

    v_lane = lax.broadcasted_iota(jnp.int32, (1, 128), 1)
    v_row = jnp.where((v_lane >= 11) & (v_lane < 14), 1.0, 0.0).astype(BF16)

    def tile(h, s, q0, tq, k0, tk, diagonal, sums):
        qs, ks = pl.ds(q0, tq), pl.ds(k0, tk)
        x = xt[h, :, qs]
        k_own = kb[s].reshape(width, hd)[k0:k0 + tk]
        v_own = vb[s].reshape(width, hd)[k0:k0 + tk]
        k_all = jnp.concatenate([k_own, fk[s, ks]], axis=1)
        v_all = jnp.concatenate([v_own, jnp.broadcast_to(v_row, (tk, 128))], axis=1)
        prob = jnp.exp2(dot(k_all, jnp.concatenate([qt[h, :, qs], x], axis=0)) * (scale * math.log2(math.e)))
        if diagonal:
            r = k0 + lax.broadcasted_iota(jnp.int32, (tk, tq), 0)
            k_pos = (r // own * 2 + core) * own + r % own
            prob = jnp.where(k_pos <= q0 + lax.broadcasted_iota(jnp.int32, (tk, tq), 1), prob, 0.0)
        dprob = dot(v_all, jnp.concatenate([gt[h, :, qs], x], axis=0))
        low = prob.astype(BF16)
        dscore = (prob * dprob).astype(BF16)
        sums[0, ks] += dot(dscore, qn[h, qs])
        sums[1, ks] += dot(low, gn[h, qs])
        dqt[h, :, qs] += dot(k_own.T, dscore)

    def to_y(s, j):
        w, to = y_peer(j)
        return remote(part_k.at[s, :, w], rs_k.at[s, j - 1], s_p.at[s], r_p.at[s], to)

    def to_z(s):
        return remote(y_out.at[s], z_in.at[s], s_q.at[s], r_q.at[s], over_z)

    def to_owner(s):
        return remote(back.at[s], fin_k.at[s], s_f.at[s], r_f.at[s], ((c + n_ctx - s) % n_ctx, t))

    def v_to_owner(s):
        return remote(part_v.at[s], fin_v.at[s], s_g.at[s], r_g.at[s], ((c + n_ctx - s) % n_ctx, t))

    def straight(i, src, dst, j):
        pz, py, to = peer(j)
        to = ((c + n_ctx - 1) % n_ctx, to[1])
        return remote(src.at[pz, py], dst.at[j], one_send.at[i], one_recv.at[i], to)

    def hand_out(s):
        part_k[s] = acc[0].astype(BF16).reshape(2, ys, own, hd)

        @pl.when(s == 1)
        def _():
            loop(0, half, lambda j: straight(0, part_k.at[1], one_k, j).start())
            out_v[...] = acc[1].astype(BF16).reshape(2, ys, own, hd)
            loop(0, half, lambda j: straight(1, out_v, one_v, j).start())

        @pl.when(s > 1)
        def _():
            loop(1, ys, lambda j: to_y(s, j).start())
            part_v[s] = acc[1].astype(BF16)
            v_to_owner(s).start()

    def sum_y(s):
        await_bytes(rs_k.at[s], r_p.at[s])

        def total(at):
            full = part_k[s, at, y].astype(F32)
            for j in range(ys - 1):
                full += rs_k[s, j, at].astype(F32)
            return full
        y_own[s] = total(z)
        y_out[s] = total(1 - z).astype(BF16)
        to_z(s).start()

    def sum_z(s):
        to_z(s).wait_recv()
        back[s] = (y_own[s] + z_in[s].astype(F32)).astype(BF16)
        to_owner(s).start()

    tq = min(256, rows)

    def edge(h, s, sums):
        for q0 in range(0, rows, tq):
            if s == 0:
                tile(h, s, q0, tq, 0, (q0 + tq) // 2, True, sums)
            else:
                tile(h, s, q0, tq, q0 // 2, width - q0 // 2, False, sums)

    acc_own[...] = jnp.zeros_like(acc_own)
    edge(1, 0, acc_own)
    pl.when(c == 0)(lambda: sib_d.start())
    down(when_has(features))

    def once(s, fn):
        if isinstance(s, int) and s >= steps:
            return

        @pl.when((c >= s) & (s < steps))
        def _():
            fn(s)

    def step(s, edged):
        @pl.when(s > ahead)
        def _():
            when_sends(wave_v)(s - ahead)
            when_has(spread_y)(s - ahead)

        @pl.when(c >= s)
        def _():
            await_bytes(part_k.at[s, :, pl.ds(0, ys - 1)], r_y.at[s])
            block_v(s).wait_recv()
            acc[...] = jnp.zeros_like(acc)
            if edged:
                edge(1, s, acc)
            else:
                tile(1, s, 0, rows, 0, width, False, acc)
            if not isinstance(s, int) or s == 1:
                @pl.when(s == 1)
                def _():
                    sib_d.start()

        once(s + 2, sum_y)
        once(s + 3, sum_z)

        @pl.when(c >= s)
        def _():
            if edged:
                edge(0, s, acc)
            else:
                tile(0, s, 0, rows, 0, width, False, acc)
            hand_out(s)

    first = steps - 1
    if first * rows == SPAN:
        step(first, True)
        first -= 1
    loop(0, first, lambda i: step(first - i, False))

    if steps > 2:
        once(2, sum_y)
    edge(0, 0, acc_own)
    out_k[...] = acc_own[0].astype(BF16).reshape(2, ys, own, hd)

    def last_k(j):
        pz, py, to = peer(j)
        return remote(out_k.at[pz, py], own_k.at[j - 1], last_send.at[0], last_recv.at[0], to)

    def last_v(j):
        pz, py, to = peer(j)
        return remote(sum_v.at[pz, py], rs_v.at[j - 1], last_send.at[1], last_recv.at[1], to)

    def collect_v(s):
        v_to_owner(s).wait_recv()
        acc_own[1] += fin_v[s].astype(F32)

    def far(fn):
        loop(0, steps - 2, lambda i: fn(steps - 1 - i))

    loop(1, half, lambda j: last_k(j).start())
    once(3, sum_z)
    once(2, sum_z)
    far(when_sends(collect_v))
    sum_v[...] = acc_own[1].astype(BF16).reshape(2, ys, own, hd)
    loop(1, half, lambda j: last_v(j).start())

    sib_d.wait_recv()
    dq_out[...] = ((dqt[0] + dqs[...]) * scale).T.astype(BF16)

    for copy in (sib_q, sib_g, sib_x, sib_d):
        copy.wait_send()

    def sent_down(s):
        along_ctx(s).wait_send()

        @pl.when(s <= ahead)
        def _():
            block_v(s).wait_send()

    def sent_near(s):
        across_z(s).wait_send()
        await_bytes(rs_k.at[s], s_y.at[s])

    def sent_up(s):
        to_owner(s).wait_send()
        v_to_owner(s).wait_send()
        await_bytes(rs_k.at[s], s_p.at[s])
        to_z(s).wait_send()

    down(when_sends(sent_down))
    down(when_has(sent_near))
    far(when_has(sent_up))

    def collect_k(s):
        to_owner(s).wait_recv()
        tot_k[...] += fin_k[s].astype(F32)

    tot_k[...] = out_k[z, y].astype(F32)
    far(when_sends(collect_k))
    for i in range(2):
        await_bytes(rs_v, near_send.at[i])

    @pl.when(c >= 1)
    def _():
        for i in range(2):
            await_bytes(one_k, one_send.at[i])

    def gathered(i, total, mine, ahead_of):
        await_bytes(rs_v, last_recv.at[i])
        for j in range(half - 1):
            total += mine[j].astype(F32)
        tot[i] = total

        @pl.when(c + 1 < n_ctx)
        def _():
            await_bytes(one_k, one_recv.at[i])
            more = ahead_of[0].astype(F32)
            for j in range(1, half):
                more += ahead_of[j].astype(F32)
            tot[i] += more

    gathered(0, tot_k[...], own_k, one_k)
    dk_out[...] = (tot[0] * scale).astype(BF16)
    gathered(1, sum_v[z, y].astype(F32), rs_v, one_v)
    dv_out[...] = tot[1].astype(BF16)
    for i in range(2):
        await_bytes(rs_v, last_send.at[i])


def body(n_ctx, n_tp, queries, keys, values, outputs, out_grad, log_norm, doc_ids):
    rows, hd = queries.shape
    own = keys.shape[0]
    half = n_tp // 2
    width = own * half
    steps = min(n_ctx, -(-SPAN // rows) + 1)
    doc_ids = doc_ids.reshape(-1, 128)
    dma = pltpu.SemaphoreType.DMA
    anywhere = pl.BlockSpec(memory_space=pl.ANY)
    inside = pl.BlockSpec(memory_space=pltpu.VMEM)
    return pl.pallas_call(
        functools.partial(kernel, n_ctx, n_tp, steps),
        out_shape=(
            jax.ShapeDtypeStruct((rows, hd), BF16),
            jax.ShapeDtypeStruct((own, hd), BF16),
            jax.ShapeDtypeStruct((own, hd), BF16),
        ),
        in_specs=[anywhere] * 7,
        out_specs=(inside, inside, inside),
        scratch_shapes=[
            pltpu.VMEM((2, rows, hd), BF16),
            pltpu.VMEM((2, rows, hd), BF16),
            pltpu.VMEM((rows, hd), BF16),
            pltpu.VMEM((2, hd, rows), BF16),
            pltpu.VMEM((2, hd, rows), BF16),
            pltpu.VMEM((2, hd, rows), BF16),
            pltpu.VMEM((steps, 2, half // 2, own, hd), BF16),
            pltpu.VMEM((steps, 2, half // 2, own, hd), BF16),
            pltpu.VMEM((steps, width, hd), BF16),
            pltpu.VMEM((2, width, hd), F32),
            pltpu.VMEM((2, hd, rows), F32),
            pltpu.VMEM((hd, rows), F32),
            pltpu.VMEM((steps, 2, half // 2, own, hd), BF16),
            pltpu.VMEM((steps, half // 2 - 1, 2, own, hd), BF16),
            pltpu.VMEM((steps, own, hd), BF16),
            pltpu.VMEM((steps, own, hd), F32),
            pltpu.VMEM((steps, own, hd), BF16),
            pltpu.VMEM((steps, own, hd), BF16),
            pltpu.VMEM((steps, own, hd), BF16),
            pltpu.VMEM((own, hd), F32),
            pltpu.VMEM((steps, width, hd), BF16),
            pltpu.VMEM((steps, width, hd), BF16),
            pltpu.VMEM((2, width, hd), F32),
            pltpu.VMEM((2, half // 2, own, hd), BF16),
            pltpu.VMEM((2, half // 2, own, hd), BF16),
            pltpu.VMEM((half - 1, own, hd), BF16),
            pltpu.VMEM((half - 1, own, hd), BF16),
            pltpu.VMEM((half, own, hd), BF16),
            pltpu.VMEM((half, own, hd), BF16),
            pltpu.VMEM((2, half // 2, own, hd), BF16),
            pltpu.VMEM((2, own, hd), F32),
            pltpu.VMEM((1, rows), F32),
            pltpu.VMEM(doc_ids.shape, jnp.int32),
            pltpu.VMEM(doc_ids.shape, jnp.int32),
            pltpu.VMEM(doc_ids.shape, jnp.int32),
            dma((7,)), dma((4,)), dma((4,)), *[dma((2,)) for _ in range(6)],
            *[dma((steps,)) for _ in range(16)],
        ],
        compiler_params=pltpu.CompilerParams(
            collective_id=0, has_side_effects=True, vmem_limit_bytes=63 * 1024 * 1024),
    )(queries, keys, values, outputs, out_grad, log_norm, doc_ids)


def solution(mesh):
    return jax.shard_map(
        functools.partial(body, mesh.shape["ctx"], mesh.shape["tp"]),
        mesh=mesh,
        in_specs=(
            P("ctx", "tp"),
            P(("ctx", "tp"), None),
            P(("ctx", "tp"), None),
            P("ctx", "tp"),
            P("ctx", "tp"),
            P("tp", "ctx"),
            P(),
        ),
        out_specs=(P("ctx", "tp"), P(("ctx", "tp"), None), P(("ctx", "tp"), None)),
        check_vma=False,
    )
```

```python
import functools
import math

import jax
import jax.numpy as jnp
from jax import lax
from jax.experimental import pallas as pl
from jax.experimental.pallas import tpu as pltpu
from jax.sharding import PartitionSpec as P

MESH = pl.DeviceIdType.MESH
SPAN = 5120
FAR = 8192.0
F32 = jnp.float32
BF16 = jnp.bfloat16


def split3(x):
    hi = x.astype(BF16).astype(F32)
    mid = (x - hi).astype(BF16).astype(F32)
    return hi, mid, x - hi - mid


def dot(a, b):
    return jnp.dot(a, b, preferred_element_type=F32)


def kernel(
    n_ctx, n_tp, steps,
    q_in, k_in, v_in, o_in, g_in, lse_in, doc_in,
    dq_out, dk_out, dv_out,
    qn, gn, on, qt, gt, xt, kb, vb, fk, acc, dqt, dqs,
    part_k, rs_k, y_out, y_own, z_in, back, fin_k, tot_k,
    part_v, fin_v, acc_own, out_k, out_v, own_k, rs_v, one_k, one_v, sum_v, tot,
    lse, doc, doc_a, doc_b,
    in_sem, sib_send, sib_recv, near_send, near_recv, last_send, last_recv, one_send, one_recv,
    s_a, r_a, s_z, r_z, s_y, r_y, s_b, r_b, s_p, r_p, s_q, r_q, s_f, r_f, s_g, r_g,
):
    rows, hd = qn.shape[1], qn.shape[2]
    half = n_tp // 2
    ys = half // 2
    own = rows // n_tp
    width = own * half
    lines = rows // 128
    scale = float(hd) ** -0.5
    c = lax.axis_index("ctx")
    t = lax.axis_index("tp")
    core = t % 2
    u = t // 2
    y = u % ys
    z = u // ys
    sib = (c, t + 1 - 2 * core)
    over_z = (c, ((1 - z) * ys + y) * 2 + core)

    loads = [
        pltpu.make_async_copy(src, dst, in_sem.at[i])
        for i, (src, dst) in enumerate((
            (k_in, kb.at[0, z, y]), (v_in, vb.at[0, z, y]), (q_in, qn.at[0]), (g_in, gn.at[0]),
            (o_in, on), (lse_in, lse), (doc_in, doc),
        ))
    ]
    for load in loads:
        load.start()

    def loop(first, last, fn):
        def one(i, _):
            fn(i)
            return 0
        lax.fori_loop(first, last, one, 0)

    def down(fn):
        loop(0, steps - 1, lambda i: fn(steps - 1 - i))

    def when_sends(fn):
        def run(s):
            @pl.when(c + s < n_ctx)
            def _():
                fn(s)
        return run

    def when_has(fn):
        def run(s):
            @pl.when(c >= s)
            def _():
                fn(s)
        return run

    def remote(src, dst, send, recv, to):
        return pltpu.make_async_remote_copy(src, dst, send, recv, to, MESH)

    def await_bytes(ref, sem):
        pltpu.make_async_copy(ref, ref, sem).wait()

    def peer(j):
        v = (u + j) % half
        return v // ys, v % ys, (c, v * 2 + core)

    def y_peer(j):
        w = (y + j) % ys
        return w, (c, (z * ys + w) * 2 + core)

    barrier = pltpu.get_barrier_semaphore()

    def greet(to):
        pl.semaphore_signal(barrier, inc=1, device_id=to, device_id_type=MESH)

    greet(sib)
    loop(1, half, lambda j: greet(peer(j)[2]))
    loop(1, n_ctx, lambda j: greet(((c + j) % n_ctx, t)))

    def near_k(j):
        return remote(kb.at[0, z, y], kb.at[0, z, y], near_send.at[0], near_recv.at[0], peer(j)[2])

    def near_v(j):
        return remote(vb.at[0, z, y], vb.at[0, z, y], near_send.at[1], near_recv.at[1], peer(j)[2])

    def along_ctx(s):
        return remote(kb.at[0, z, y], kb.at[s, z, y], s_a.at[s], r_a.at[s], ((c + s) % n_ctx, t))

    def across_z(s):
        return remote(kb.at[s, z, y], kb.at[s, z, y], s_z.at[s], r_z.at[s], over_z)

    def along_y(s, j):
        return remote(kb.at[s, :, y], kb.at[s, :, y], s_y.at[s], r_y.at[s], y_peer(j)[1])

    def block_v(s):
        return remote(vb.at[0], vb.at[s], s_b.at[s], r_b.at[s], ((c + s) % n_ctx, t))

    sib_q = remote(qn.at[0], qn.at[1], sib_send.at[0], sib_recv.at[0], sib)
    sib_g = remote(gn.at[0], gn.at[1], sib_send.at[1], sib_recv.at[1], sib)
    sib_x = remote(xt.at[0, pl.ds(0, 16)], xt.at[1, pl.ds(0, 16)], sib_send.at[2], sib_recv.at[2], sib)
    sib_d = remote(dqt.at[1], dqs, sib_send.at[3], sib_recv.at[3], sib)

    for load in loads[:2]:
        load.wait()
    pl.semaphore_wait(barrier, 1 + half - 1 + n_ctx - 1)
    down(when_sends(lambda s: along_ctx(s).start()))
    loop(1, half, lambda j: near_v(j).start())
    for load in loads[2:4]:
        load.wait()
    sib_q.start()
    sib_g.start()
    loop(1, half, lambda j: near_k(j).start())
    for load in loads[4:]:
        load.wait()
    q_doc = jnp.concatenate([doc[pl.ds(c * lines + j, 1), :] for j in range(lines)], axis=1)
    delta = jnp.sum(gn[0].T.astype(F32) * on[...].T.astype(F32), axis=0, keepdims=True)
    place = lax.broadcasted_iota(jnp.int32, (8, rows), 0)
    extra = jnp.zeros((8, rows), F32)
    for i, row in enumerate((*split3(lse[...] * math.sqrt(hd)), *split3(delta))):
        extra = jnp.where(place == i, -row, extra)
    xt[0, 0:8, :] = jnp.where(place == q_doc, -FAR, 0.0).astype(BF16)
    xt[0, 8:16, :] = extra.astype(BF16)

    sib_x.start()

    qt[0] = qn[0].T
    gt[0] = gn[0].T
    for h in range(2):
        xt[h, 16:, :] = jnp.zeros((hd - 16, rows), BF16)
    dqt[...] = jnp.zeros_like(dqt)
    turned = pltpu.roll(doc[...], 64, 1)
    doc_a[...] = jnp.where(core == 0, doc[...], turned)
    doc_b[...] = jnp.where(core == 0, turned, doc[...])
    lane = lax.broadcasted_iota(jnp.int32, (128, 128), 1)

    def features(s):
        for m in range(lines // 2):
            at = (c - s) * lines + 2 * m
            both = jnp.where(lane < 64, doc_a[pl.ds(at, 1), :], doc_b[pl.ds(at + 1, 1), :])
            other = jnp.where((lane < 11) & (both.T != lane), 1.0, 0.0)
            fk[s, m * 128:(m + 1) * 128, :] = other.astype(BF16)

    features(0)
    down(when_has(lambda s: along_ctx(s).wait_recv()))
    down(when_has(lambda s: across_z(s).start()))
    sib_x.wait_recv()
    sib_q.wait_recv()
    sib_g.wait_recv()
    qt[1] = qn[1].T
    gt[1] = gn[1].T

    await_bytes(rs_v, near_recv.at[1])

    def spread_y(s):
        across_z(s).wait_recv()
        loop(1, ys, lambda j: along_y(s, j).start())

    ahead = 2

    def wave_v(s):
        @pl.when((c + s + ahead < n_ctx) & (s + ahead < steps))
        def _():
            block_v(s + ahead).wait_send()
        block_v(s).start()

    lead = max(steps - 1 - ahead, 0)
    loop(0, steps - 1 - lead, lambda i: when_sends(wave_v)(steps - 1 - i))
    down(when_has(spread_y))
    await_bytes(rs_v, near_recv.at[0])

    v_lane = lax.broadcasted_iota(jnp.int32, (1, 128), 1)
    v_row = jnp.where((v_lane >= 11) & (v_lane < 14), 1.0, 0.0).astype(BF16)

    def tile(h, s, q0, tq, k0, tk, diagonal, sums):
        qs, ks = pl.ds(q0, tq), pl.ds(k0, tk)
        x = xt[h, :, qs]
        k_own = kb[s].reshape(width, hd)[k0:k0 + tk]
        v_own = vb[s].reshape(width, hd)[k0:k0 + tk]
        k_all = jnp.concatenate([k_own, fk[s, ks]], axis=1)
        v_all = jnp.concatenate([v_own, jnp.broadcast_to(v_row, (tk, 128))], axis=1)
        prob = jnp.exp2(dot(k_all, jnp.concatenate([qt[h, :, qs], x], axis=0)) * (scale * math.log2(math.e)))
        if diagonal:
            r = k0 + lax.broadcasted_iota(jnp.int32, (tk, tq), 0)
            k_pos = (r // own * 2 + core) * own + r % own
            prob = jnp.where(k_pos <= q0 + lax.broadcasted_iota(jnp.int32, (tk, tq), 1), prob, 0.0)
        dprob = dot(v_all, jnp.concatenate([gt[h, :, qs], x], axis=0))
        low = prob.astype(BF16)
        dscore = (prob * dprob).astype(BF16)
        sums[0, ks] += dot(dscore, qn[h, qs])
        sums[1, ks] += dot(low, gn[h, qs])
        dqt[h, :, qs] += dot(k_own.T, dscore)

    def to_y(s, j):
        w, to = y_peer(j)
        return remote(part_k.at[s, :, w], rs_k.at[s, j - 1], s_p.at[s], r_p.at[s], to)

    def to_z(s):
        return remote(y_out.at[s], z_in.at[s], s_q.at[s], r_q.at[s], over_z)

    def to_owner(s):
        return remote(back.at[s], fin_k.at[s], s_f.at[s], r_f.at[s], ((c + n_ctx - s) % n_ctx, t))

    def v_to_owner(s):
        return remote(part_v.at[s], fin_v.at[s], s_g.at[s], r_g.at[s], ((c + n_ctx - s) % n_ctx, t))

    def straight(i, src, dst, j):
        pz, py, to = peer(j)
        to = ((c + n_ctx - 1) % n_ctx, to[1])
        return remote(src.at[pz, py], dst.at[j], one_send.at[i], one_recv.at[i], to)

    def hand_out(s):
        part_k[s] = acc[0].astype(BF16).reshape(2, ys, own, hd)

        @pl.when(s == 1)
        def _():
            loop(0, half, lambda j: straight(0, part_k.at[1], one_k, j).start())
            out_v[...] = acc[1].astype(BF16).reshape(2, ys, own, hd)
            loop(0, half, lambda j: straight(1, out_v, one_v, j).start())

        @pl.when(s > 1)
        def _():
            loop(1, ys, lambda j: to_y(s, j).start())
            part_v[s] = acc[1].astype(BF16)
            v_to_owner(s).start()

    def sum_y(s):
        await_bytes(rs_k.at[s], r_p.at[s])

        def total(at):
            full = part_k[s, at, y].astype(F32)
            for j in range(ys - 1):
                full += rs_k[s, j, at].astype(F32)
            return full
        y_own[s] = total(z)
        y_out[s] = total(1 - z).astype(BF16)
        to_z(s).start()

    def sum_z(s):
        to_z(s).wait_recv()
        back[s] = (y_own[s] + z_in[s].astype(F32)).astype(BF16)
        to_owner(s).start()

    tq = min(256, rows)

    def edge(h, s, sums):
        for q0 in range(0, rows, tq):
            if s == 0:
                tile(h, s, q0, tq, 0, (q0 + tq) // 2, True, sums)
            else:
                tile(h, s, q0, tq, q0 // 2, width - q0 // 2, False, sums)

    acc_own[...] = jnp.zeros_like(acc_own)
    edge(1, 0, acc_own)
    pl.when(c == 0)(lambda: sib_d.start())
    edge(0, 0, acc_own)
    out_k[...] = acc_own[0].astype(BF16).reshape(2, ys, own, hd)

    def last_k(j):
        pz, py, to = peer(j)
        return remote(out_k.at[pz, py], own_k.at[j - 1], last_send.at[0], last_recv.at[0], to)

    def last_v(j):
        pz, py, to = peer(j)
        return remote(sum_v.at[pz, py], rs_v.at[j - 1], last_send.at[1], last_recv.at[1], to)

    loop(1, half, lambda j: last_k(j).start())
    down(when_has(features))

    def once(s, fn):
        if isinstance(s, int) and s >= steps:
            return

        @pl.when((c >= s) & (s < steps))
        def _():
            fn(s)

    def step(s, edged):
        @pl.when(s > ahead)
        def _():
            when_sends(wave_v)(s - ahead)

        @pl.when(c >= s)
        def _():
            await_bytes(part_k.at[s, :, pl.ds(0, ys - 1)], r_y.at[s])
            block_v(s).wait_recv()
            acc[...] = jnp.zeros_like(acc)
            if edged:
                edge(1, s, acc)
            else:
                tile(1, s, 0, rows, 0, width, False, acc)
            if not isinstance(s, int) or s == 1:
                @pl.when(s == 1)
                def _():
                    sib_d.start()

        once(s + 2, sum_y)
        once(s + 3, sum_z)

        @pl.when(c >= s)
        def _():
            if edged:
                edge(0, s, acc)
            else:
                tile(0, s, 0, rows, 0, width, False, acc)
            hand_out(s)

    first = steps - 1
    if first * rows == SPAN:
        step(first, True)
        first -= 1
    loop(0, first, lambda i: step(first - i, False))

    if steps > 2:
        once(2, sum_y)
    def collect_v(s):
        v_to_owner(s).wait_recv()
        acc_own[1] += fin_v[s].astype(F32)

    def far(fn):
        loop(0, steps - 2, lambda i: fn(steps - 1 - i))

    once(3, sum_z)
    far(when_sends(collect_v))
    sum_v[...] = acc_own[1].astype(BF16).reshape(2, ys, own, hd)
    loop(1, half, lambda j: last_v(j).start())
    once(2, sum_z)

    sib_d.wait_recv()
    dq_out[...] = ((dqt[0] + dqs[...]) * scale).T.astype(BF16)

    for copy in (sib_q, sib_g, sib_x, sib_d):
        copy.wait_send()

    def sent_down(s):
        along_ctx(s).wait_send()

        @pl.when(s <= ahead)
        def _():
            block_v(s).wait_send()

    def sent_near(s):
        across_z(s).wait_send()
        await_bytes(rs_k.at[s], s_y.at[s])

    def sent_up(s):
        to_owner(s).wait_send()
        v_to_owner(s).wait_send()
        await_bytes(rs_k.at[s], s_p.at[s])
        to_z(s).wait_send()

    down(when_sends(sent_down))
    down(when_has(sent_near))
    far(when_has(sent_up))

    def collect_k(s):
        to_owner(s).wait_recv()
        tot_k[...] += fin_k[s].astype(F32)

    tot_k[...] = out_k[z, y].astype(F32)
    far(when_sends(collect_k))
    for i in range(2):
        await_bytes(rs_v, near_send.at[i])

    @pl.when(c >= 1)
    def _():
        for i in range(2):
            await_bytes(one_k, one_send.at[i])

    def gathered(i, total, mine, ahead_of):
        await_bytes(rs_v, last_recv.at[i])
        for j in range(half - 1):
            total += mine[j].astype(F32)
        tot[i] = total

        @pl.when(c + 1 < n_ctx)
        def _():
            await_bytes(one_k, one_recv.at[i])
            more = ahead_of[0].astype(F32)
            for j in range(1, half):
                more += ahead_of[j].astype(F32)
            tot[i] += more

    gathered(0, tot_k[...], own_k, one_k)
    dk_out[...] = (tot[0] * scale).astype(BF16)
    gathered(1, sum_v[z, y].astype(F32), rs_v, one_v)
    dv_out[...] = tot[1].astype(BF16)
    for i in range(2):
        await_bytes(rs_v, last_send.at[i])


def hand_over(*refs):
    half = len(refs) // 2
    for src, dst in zip(refs[:half], refs[half:]):
        dst[...] = src[...]


def body(n_ctx, n_tp, queries, keys, values, outputs, out_grad, log_norm, doc_ids):
    rows, hd = queries.shape
    own = keys.shape[0]
    half = n_tp // 2
    width = own * half
    steps = min(n_ctx, -(-SPAN // rows) + 1)
    doc_ids = doc_ids.reshape(-1, 128)
    dma = pltpu.SemaphoreType.DMA
    anywhere = pl.BlockSpec(memory_space=pl.ANY)
    inside = pl.BlockSpec(memory_space=pltpu.VMEM)
    grads = pl.pallas_call(
        functools.partial(kernel, n_ctx, n_tp, steps),
        out_shape=(
            jax.ShapeDtypeStruct((rows, hd), BF16),
            jax.ShapeDtypeStruct((own, hd), BF16),
            jax.ShapeDtypeStruct((own, hd), BF16),
        ),
        in_specs=[anywhere] * 7,
        out_specs=(inside, inside, inside),
        scratch_shapes=[
            pltpu.VMEM((2, rows, hd), BF16),
            pltpu.VMEM((2, rows, hd), BF16),
            pltpu.VMEM((rows, hd), BF16),
            pltpu.VMEM((2, hd, rows), BF16),
            pltpu.VMEM((2, hd, rows), BF16),
            pltpu.VMEM((2, hd, rows), BF16),
            pltpu.VMEM((steps, 2, half // 2, own, hd), BF16),
            pltpu.VMEM((steps, 2, half // 2, own, hd), BF16),
            pltpu.VMEM((steps, width, hd), BF16),
            pltpu.VMEM((2, width, hd), F32),
            pltpu.VMEM((2, hd, rows), F32),
            pltpu.VMEM((hd, rows), F32),
            pltpu.VMEM((steps, 2, half // 2, own, hd), BF16),
            pltpu.VMEM((steps, half // 2 - 1, 2, own, hd), BF16),
            pltpu.VMEM((steps, own, hd), BF16),
            pltpu.VMEM((steps, own, hd), F32),
            pltpu.VMEM((steps, own, hd), BF16),
            pltpu.VMEM((steps, own, hd), BF16),
            pltpu.VMEM((steps, own, hd), BF16),
            pltpu.VMEM((own, hd), F32),
            pltpu.VMEM((steps, width, hd), BF16),
            pltpu.VMEM((steps, width, hd), BF16),
            pltpu.VMEM((2, width, hd), F32),
            pltpu.VMEM((2, half // 2, own, hd), BF16),
            pltpu.VMEM((2, half // 2, own, hd), BF16),
            pltpu.VMEM((half - 1, own, hd), BF16),
            pltpu.VMEM((half - 1, own, hd), BF16),
            pltpu.VMEM((half, own, hd), BF16),
            pltpu.VMEM((half, own, hd), BF16),
            pltpu.VMEM((2, half // 2, own, hd), BF16),
            pltpu.VMEM((2, own, hd), F32),
            pltpu.VMEM((1, rows), F32),
            pltpu.VMEM(doc_ids.shape, jnp.int32),
            pltpu.VMEM(doc_ids.shape, jnp.int32),
            pltpu.VMEM(doc_ids.shape, jnp.int32),
            dma((7,)), dma((4,)), dma((4,)), *[dma((2,)) for _ in range(6)],
            *[dma((steps,)) for _ in range(16)],
        ],
        compiler_params=pltpu.CompilerParams(
            collective_id=0, has_side_effects=True, vmem_limit_bytes=63 * 1024 * 1024),
    )(queries, keys, values, outputs, out_grad, log_norm, doc_ids)
    return pl.pallas_call(
        hand_over,
        out_shape=tuple(jax.ShapeDtypeStruct(x.shape, x.dtype) for x in grads),
        in_specs=[inside] * 3,
        out_specs=(inside,) * 3,
    )(*grads)


def solution(mesh):
    return jax.shard_map(
        functools.partial(body, mesh.shape["ctx"], mesh.shape["tp"]),
        mesh=mesh,
        in_specs=(
            P("ctx", "tp"),
            P(("ctx", "tp"), None),
            P(("ctx", "tp"), None),
            P("ctx", "tp"),
            P("ctx", "tp"),
            P("tp", "ctx"),
            P(),
        ),
        out_specs=(P("ctx", "tp"), P(("ctx", "tp"), None), P(("ctx", "tp"), None)),
        check_vma=False,
    )
```

```python
import functools
import math

import jax
import jax.numpy as jnp
from jax import lax
from jax.experimental import pallas as pl
from jax.experimental.pallas import tpu as pltpu
from jax.sharding import PartitionSpec as P

MESH = pl.DeviceIdType.MESH
SPAN = 5120
FAR = 8192.0
F32 = jnp.float32
BF16 = jnp.bfloat16


def split3(x):
    hi = x.astype(BF16).astype(F32)
    mid = (x - hi).astype(BF16).astype(F32)
    return hi, mid, x - hi - mid


def dot(a, b):
    return jnp.dot(a, b, preferred_element_type=F32)


def kernel(
    n_ctx, n_tp, steps,
    q_in, k_in, v_in, o_in, g_in, lse_in, doc_in,
    dq_out, dk_out, dv_out,
    qn, gn, on, qt, gt, xt, kb, vb, fk, acc, dqt, dqs,
    part_k, rs_k, y_out, y_own, z_in, back, fin_k, tot_k,
    part_v, fin_v, acc_own, out_k, out_v, own_k, rs_v, one_k, one_v, sum_v, tot,
    lse, doc, doc_a, doc_b,
    in_sem, sib_send, sib_recv, near_send, near_recv, last_send, last_recv, one_send, one_recv,
    s_a, r_a, s_z, r_z, s_y, r_y, s_b, r_b, s_p, r_p, s_q, r_q, s_f, r_f, s_g, r_g,
):
    rows, hd = qn.shape[1], qn.shape[2]
    half = n_tp // 2
    ys = half // 2
    own = rows // n_tp
    width = own * half
    lines = rows // 128
    scale = float(hd) ** -0.5
    c = lax.axis_index("ctx")
    t = lax.axis_index("tp")
    core = t % 2
    u = t // 2
    y = u % ys
    z = u // ys
    sib = (c, t + 1 - 2 * core)
    over_z = (c, ((1 - z) * ys + y) * 2 + core)

    loads = [
        pltpu.make_async_copy(src, dst, in_sem.at[i])
        for i, (src, dst) in enumerate((
            (k_in, kb.at[0, z, y]), (v_in, vb.at[0, z, y]), (q_in, qn.at[0]), (g_in, gn.at[0]),
            (o_in, on), (lse_in, lse), (doc_in, doc),
        ))
    ]
    for load in loads:
        load.start()

    def loop(first, last, fn):
        def one(i, _):
            fn(i)
            return 0
        lax.fori_loop(first, last, one, 0)

    def down(fn):
        loop(0, steps - 1, lambda i: fn(steps - 1 - i))

    def when_sends(fn):
        def run(s):
            @pl.when(c + s < n_ctx)
            def _():
                fn(s)
        return run

    def when_has(fn):
        def run(s):
            @pl.when(c >= s)
            def _():
                fn(s)
        return run

    def remote(src, dst, send, recv, to):
        return pltpu.make_async_remote_copy(src, dst, send, recv, to, MESH)

    def await_bytes(ref, sem):
        pltpu.make_async_copy(ref, ref, sem).wait()

    def peer(j):
        v = (u + j) % half
        return v // ys, v % ys, (c, v * 2 + core)

    def y_peer(j):
        w = (y + j) % ys
        return w, (c, (z * ys + w) * 2 + core)

    barrier = pltpu.get_barrier_semaphore()

    def greet(to):
        pl.semaphore_signal(barrier, inc=1, device_id=to, device_id_type=MESH)

    greet(sib)
    loop(1, half, lambda j: greet(peer(j)[2]))
    loop(1, n_ctx, lambda j: greet(((c + j) % n_ctx, t)))

    def near_k(j):
        return remote(kb.at[0, z, y], kb.at[0, z, y], near_send.at[0], near_recv.at[0], peer(j)[2])

    def near_v(j):
        return remote(vb.at[0, z, y], vb.at[0, z, y], near_send.at[1], near_recv.at[1], peer(j)[2])

    def along_ctx(s):
        return remote(kb.at[0, z, y], kb.at[s, z, y], s_a.at[s], r_a.at[s], ((c + s) % n_ctx, t))

    def across_z(s):
        return remote(kb.at[s, z, y], kb.at[s, z, y], s_z.at[s], r_z.at[s], over_z)

    def along_y(s, j):
        return remote(kb.at[s, :, y], kb.at[s, :, y], s_y.at[s], r_y.at[s], y_peer(j)[1])

    def block_v(s):
        return remote(vb.at[0], vb.at[s], s_b.at[s], r_b.at[s], ((c + s) % n_ctx, t))

    sib_q = remote(qn.at[0], qn.at[1], sib_send.at[0], sib_recv.at[0], sib)
    sib_g = remote(gn.at[0], gn.at[1], sib_send.at[1], sib_recv.at[1], sib)
    sib_x = remote(xt.at[0, pl.ds(0, 16)], xt.at[1, pl.ds(0, 16)], sib_send.at[2], sib_recv.at[2], sib)
    sib_d = remote(dqt.at[1], dqs, sib_send.at[3], sib_recv.at[3], sib)

    for load in loads[:2]:
        load.wait()
    pl.semaphore_wait(barrier, 1 + half - 1 + n_ctx - 1)
    down(when_sends(lambda s: along_ctx(s).start()))
    loop(1, half, lambda j: near_v(j).start())
    for load in loads[2:4]:
        load.wait()
    sib_q.start()
    sib_g.start()
    loop(1, half, lambda j: near_k(j).start())
    for load in loads[4:]:
        load.wait()
    q_doc = jnp.concatenate([doc[pl.ds(c * lines + j, 1), :] for j in range(lines)], axis=1)
    delta = jnp.sum(gn[0].T.astype(F32) * on[...].T.astype(F32), axis=0, keepdims=True)
    place = lax.broadcasted_iota(jnp.int32, (8, rows), 0)
    extra = jnp.zeros((8, rows), F32)
    for i, row in enumerate((*split3(lse[...] * math.sqrt(hd)), *split3(delta))):
        extra = jnp.where(place == i, -row, extra)
    xt[0, 0:8, :] = jnp.where(place == q_doc, -FAR, 0.0).astype(BF16)
    xt[0, 8:16, :] = extra.astype(BF16)

    sib_x.start()

    qt[0] = qn[0].T
    gt[0] = gn[0].T
    for h in range(2):
        xt[h, 16:, :] = jnp.zeros((hd - 16, rows), BF16)
    dqt[...] = jnp.zeros_like(dqt)
    turned = pltpu.roll(doc[...], 64, 1)
    doc_a[...] = jnp.where(core == 0, doc[...], turned)
    doc_b[...] = jnp.where(core == 0, turned, doc[...])
    lane = lax.broadcasted_iota(jnp.int32, (128, 128), 1)

    def features(s):
        for m in range(lines // 2):
            at = (c - s) * lines + 2 * m
            both = jnp.where(lane < 64, doc_a[pl.ds(at, 1), :], doc_b[pl.ds(at + 1, 1), :])
            other = jnp.where((lane < 11) & (both.T != lane), 1.0, 0.0)
            fk[s, m * 128:(m + 1) * 128, :] = other.astype(BF16)

    features(0)
    down(when_has(lambda s: along_ctx(s).wait_recv()))
    down(when_has(lambda s: across_z(s).start()))
    sib_x.wait_recv()
    sib_q.wait_recv()
    sib_g.wait_recv()
    qt[1] = qn[1].T
    gt[1] = gn[1].T

    await_bytes(rs_v, near_recv.at[1])

    def spread_y(s):
        across_z(s).wait_recv()
        loop(1, ys, lambda j: along_y(s, j).start())

    ahead = 2

    def wave_v(s):
        @pl.when((c + s + ahead < n_ctx) & (s + ahead < steps))
        def _():
            block_v(s + ahead).wait_send()
        block_v(s).start()

    lead = max(steps - 1 - ahead, 0)
    loop(0, steps - 1 - lead, lambda i: when_sends(wave_v)(steps - 1 - i))
    down(when_has(spread_y))
    down(when_has(features))
    await_bytes(rs_v, near_recv.at[0])

    v_lane = lax.broadcasted_iota(jnp.int32, (1, 128), 1)
    v_row = jnp.where((v_lane >= 11) & (v_lane < 14), 1.0, 0.0).astype(BF16)

    def tile(h, s, q0, tq, k0, tk, diagonal, sums):
        qs, ks = pl.ds(q0, tq), pl.ds(k0, tk)
        x = xt[h, :, qs]
        k_own = kb[s].reshape(width, hd)[k0:k0 + tk]
        v_own = vb[s].reshape(width, hd)[k0:k0 + tk]
        k_all = jnp.concatenate([k_own, fk[s, ks]], axis=1)
        v_all = jnp.concatenate([v_own, jnp.broadcast_to(v_row, (tk, 128))], axis=1)
        prob = jnp.exp2(dot(k_all, jnp.concatenate([qt[h, :, qs], x], axis=0)) * (scale * math.log2(math.e)))
        if diagonal:
            r = k0 + lax.broadcasted_iota(jnp.int32, (tk, tq), 0)
            k_pos = (r // own * 2 + core) * own + r % own
            prob = jnp.where(k_pos <= q0 + lax.broadcasted_iota(jnp.int32, (tk, tq), 1), prob, 0.0)
        dprob = dot(v_all, jnp.concatenate([gt[h, :, qs], x], axis=0))
        low = prob.astype(BF16)
        dscore = (prob * dprob).astype(BF16)
        sums[0, ks] += dot(dscore, qn[h, qs])
        sums[1, ks] += dot(low, gn[h, qs])
        dqt[h, :, qs] += dot(k_own.T, dscore)

    def to_y(s, j):
        w, to = y_peer(j)
        return remote(part_k.at[s, :, w], rs_k.at[s, j - 1], s_p.at[s], r_p.at[s], to)

    def to_z(s):
        return remote(y_out.at[s], z_in.at[s], s_q.at[s], r_q.at[s], over_z)

    def to_owner(s):
        return remote(back.at[s], fin_k.at[s], s_f.at[s], r_f.at[s], ((c + n_ctx - s) % n_ctx, t))

    def v_to_owner(s):
        return remote(part_v.at[s], fin_v.at[s], s_g.at[s], r_g.at[s], ((c + n_ctx - s) % n_ctx, t))

    def straight(i, src, dst, j):
        pz, py, to = peer(j)
        to = ((c + n_ctx - 1) % n_ctx, to[1])
        return remote(src.at[pz, py], dst.at[j], one_send.at[i], one_recv.at[i], to)

    def hand_out(s):
        part_k[s] = acc[0].astype(BF16).reshape(2, ys, own, hd)

        @pl.when(s == 1)
        def _():
            loop(0, half, lambda j: straight(0, part_k.at[1], one_k, j).start())
            out_v[...] = acc[1].astype(BF16).reshape(2, ys, own, hd)
            loop(0, half, lambda j: straight(1, out_v, one_v, j).start())

        @pl.when(s > 1)
        def _():
            part_v[s] = acc[1].astype(BF16)
            v_to_owner(s).start()
            loop(1, ys, lambda j: to_y(s, j).start())

    def sum_y(s):
        await_bytes(rs_k.at[s], r_p.at[s])

        def total(at):
            full = part_k[s, at, y].astype(F32)
            for j in range(ys - 1):
                full += rs_k[s, j, at].astype(F32)
            return full
        y_own[s] = total(z)
        y_out[s] = total(1 - z).astype(BF16)
        to_z(s).start()

    def sum_z(s):
        to_z(s).wait_recv()
        back[s] = (y_own[s] + z_in[s].astype(F32)).astype(BF16)
        to_owner(s).start()

    tq = min(256, rows)

    def edge(h, s, sums):
        for q0 in range(0, rows, tq):
            if s == 0:
                tile(h, s, q0, tq, 0, (q0 + tq) // 2, True, sums)
            else:
                tile(h, s, q0, tq, q0 // 2, width - q0 // 2, False, sums)

    acc_own[...] = jnp.zeros_like(acc_own)
    edge(1, 0, acc_own)
    pl.when(c == 0)(lambda: sib_d.start())
    edge(0, 0, acc_own)
    out_k[...] = acc_own[0].astype(BF16).reshape(2, ys, own, hd)

    def last_k(j):
        pz, py, to = peer(j)
        return remote(out_k.at[pz, py], own_k.at[j - 1], last_send.at[0], last_recv.at[0], to)

    def last_v(j):
        pz, py, to = peer(j)
        return remote(sum_v.at[pz, py], rs_v.at[j - 1], last_send.at[1], last_recv.at[1], to)

    loop(1, half, lambda j: last_k(j).start())

    def once(s, fn):
        if isinstance(s, int) and s >= steps:
            return

        @pl.when((c >= s) & (s < steps))
        def _():
            fn(s)

    def step(s, edged):
        @pl.when(s > ahead)
        def _():
            when_sends(wave_v)(s - ahead)

        @pl.when(c >= s)
        def _():
            await_bytes(part_k.at[s, :, pl.ds(0, ys - 1)], r_y.at[s])
            block_v(s).wait_recv()
            acc[...] = jnp.zeros_like(acc)
            if edged:
                edge(1, s, acc)
            else:
                tile(1, s, 0, rows, 0, width, False, acc)
            if not isinstance(s, int) or s == 1:
                @pl.when(s == 1)
                def _():
                    sib_d.start()

        once(s + 2, sum_y)
        once(s + 3, sum_z)

        @pl.when(c >= s)
        def _():
            if edged:
                edge(0, s, acc)
            else:
                tile(0, s, 0, rows, 0, width, False, acc)
            hand_out(s)

    first = steps - 1
    if first * rows == SPAN:
        step(first, True)
        first -= 1
    loop(0, first, lambda i: step(first - i, False))

    if steps > 2:
        once(2, sum_y)
    def collect_v(s):
        v_to_owner(s).wait_recv()
        acc_own[1] += fin_v[s].astype(F32)

    def far(fn):
        loop(0, steps - 2, lambda i: fn(steps - 1 - i))

    far(when_sends(collect_v))
    sum_v[...] = acc_own[1].astype(BF16).reshape(2, ys, own, hd)
    loop(1, half, lambda j: last_v(j).start())
    once(3, sum_z)
    once(2, sum_z)

    sib_d.wait_recv()
    dq_out[...] = ((dqt[0] + dqs[...]) * scale).T.astype(BF16)

    for copy in (sib_q, sib_g, sib_x, sib_d):
        copy.wait_send()

    def sent_down(s):
        along_ctx(s).wait_send()

        @pl.when(s <= ahead)
        def _():
            block_v(s).wait_send()

    def sent_near(s):
        across_z(s).wait_send()
        await_bytes(rs_k.at[s], s_y.at[s])

    def sent_up(s):
        to_owner(s).wait_send()
        v_to_owner(s).wait_send()
        await_bytes(rs_k.at[s], s_p.at[s])
        to_z(s).wait_send()

    down(when_sends(sent_down))
    down(when_has(sent_near))
    far(when_has(sent_up))

    def collect_k(s):
        to_owner(s).wait_recv()
        tot_k[...] += fin_k[s].astype(F32)

    tot_k[...] = out_k[z, y].astype(F32)
    far(when_sends(collect_k))
    for i in range(2):
        await_bytes(rs_v, near_send.at[i])

    @pl.when(c >= 1)
    def _():
        for i in range(2):
            await_bytes(one_k, one_send.at[i])

    def gathered(i, total, mine, ahead_of):
        await_bytes(rs_v, last_recv.at[i])
        for j in range(half - 1):
            total += mine[j].astype(F32)
        tot[i] = total

        @pl.when(c + 1 < n_ctx)
        def _():
            await_bytes(one_k, one_recv.at[i])
            more = ahead_of[0].astype(F32)
            for j in range(1, half):
                more += ahead_of[j].astype(F32)
            tot[i] += more

    gathered(0, tot_k[...], own_k, one_k)
    dk_out[...] = (tot[0] * scale).astype(BF16)
    gathered(1, sum_v[z, y].astype(F32), rs_v, one_v)
    dv_out[...] = tot[1].astype(BF16)
    for i in range(2):
        await_bytes(rs_v, last_send.at[i])


def hand_over(*refs):
    half = len(refs) // 2
    for src, dst in zip(refs[:half], refs[half:]):
        dst[...] = src[...]


def body(n_ctx, n_tp, queries, keys, values, outputs, out_grad, log_norm, doc_ids):
    rows, hd = queries.shape
    own = keys.shape[0]
    half = n_tp // 2
    width = own * half
    steps = min(n_ctx, -(-SPAN // rows) + 1)
    doc_ids = doc_ids.reshape(-1, 128)
    dma = pltpu.SemaphoreType.DMA
    anywhere = pl.BlockSpec(memory_space=pl.ANY)
    inside = pl.BlockSpec(memory_space=pltpu.VMEM)
    grads = pl.pallas_call(
        functools.partial(kernel, n_ctx, n_tp, steps),
        out_shape=(
            jax.ShapeDtypeStruct((rows, hd), BF16),
            jax.ShapeDtypeStruct((own, hd), BF16),
            jax.ShapeDtypeStruct((own, hd), BF16),
        ),
        in_specs=[anywhere] * 7,
        out_specs=(inside, inside, inside),
        scratch_shapes=[
            pltpu.VMEM((2, rows, hd), BF16),
            pltpu.VMEM((2, rows, hd), BF16),
            pltpu.VMEM((rows, hd), BF16),
            pltpu.VMEM((2, hd, rows), BF16),
            pltpu.VMEM((2, hd, rows), BF16),
            pltpu.VMEM((2, hd, rows), BF16),
            pltpu.VMEM((steps, 2, half // 2, own, hd), BF16),
            pltpu.VMEM((steps, 2, half // 2, own, hd), BF16),
            pltpu.VMEM((steps, width, hd), BF16),
            pltpu.VMEM((2, width, hd), F32),
            pltpu.VMEM((2, hd, rows), F32),
            pltpu.VMEM((hd, rows), F32),
            pltpu.VMEM((steps, 2, half // 2, own, hd), BF16),
            pltpu.VMEM((steps, half // 2 - 1, 2, own, hd), BF16),
            pltpu.VMEM((steps, own, hd), BF16),
            pltpu.VMEM((steps, own, hd), F32),
            pltpu.VMEM((steps, own, hd), BF16),
            pltpu.VMEM((steps, own, hd), BF16),
            pltpu.VMEM((steps, own, hd), BF16),
            pltpu.VMEM((own, hd), F32),
            pltpu.VMEM((steps, width, hd), BF16),
            pltpu.VMEM((steps, width, hd), BF16),
            pltpu.VMEM((2, width, hd), F32),
            pltpu.VMEM((2, half // 2, own, hd), BF16),
            pltpu.VMEM((2, half // 2, own, hd), BF16),
            pltpu.VMEM((half - 1, own, hd), BF16),
            pltpu.VMEM((half - 1, own, hd), BF16),
            pltpu.VMEM((half, own, hd), BF16),
            pltpu.VMEM((half, own, hd), BF16),
            pltpu.VMEM((2, half // 2, own, hd), BF16),
            pltpu.VMEM((2, own, hd), F32),
            pltpu.VMEM((1, rows), F32),
            pltpu.VMEM(doc_ids.shape, jnp.int32),
            pltpu.VMEM(doc_ids.shape, jnp.int32),
            pltpu.VMEM(doc_ids.shape, jnp.int32),
            dma((7,)), dma((4,)), dma((4,)), *[dma((2,)) for _ in range(6)],
            *[dma((steps,)) for _ in range(16)],
        ],
        compiler_params=pltpu.CompilerParams(
            collective_id=0, has_side_effects=True, vmem_limit_bytes=63 * 1024 * 1024),
    )(queries, keys, values, outputs, out_grad, log_norm, doc_ids)
    return pl.pallas_call(
        hand_over,
        out_shape=tuple(jax.ShapeDtypeStruct(x.shape, x.dtype) for x in grads),
        in_specs=[inside] * 3,
        out_specs=(inside,) * 3,
    )(*grads)


def solution(mesh):
    return jax.shard_map(
        functools.partial(body, mesh.shape["ctx"], mesh.shape["tp"]),
        mesh=mesh,
        in_specs=(
            P("ctx", "tp"),
            P(("ctx", "tp"), None),
            P(("ctx", "tp"), None),
            P("ctx", "tp"),
            P("ctx", "tp"),
            P("tp", "ctx"),
            P(),
        ),
        out_specs=(P("ctx", "tp"), P(("ctx", "tp"), None), P(("ctx", "tp"), None)),
        check_vma=False,
    )
```

```python
import functools
import math

import jax
import jax.numpy as jnp
from jax import lax
from jax.experimental import pallas as pl
from jax.experimental.pallas import tpu as pltpu
from jax.sharding import PartitionSpec as P

MESH = pl.DeviceIdType.MESH
SPAN = 5120
FAR = 8192.0
F32 = jnp.float32
BF16 = jnp.bfloat16


def split3(x):
    hi = x.astype(BF16).astype(F32)
    mid = (x - hi).astype(BF16).astype(F32)
    return hi, mid, x - hi - mid


def dot(a, b):
    return jnp.dot(a, b, preferred_element_type=F32)


def kernel(
    n_ctx, n_tp, steps,
    q_in, k_in, v_in, o_in, g_in, lse_in, doc_in,
    dq_out, dk_out, dv_out,
    qn, gn, on, qt, gt, xt, kb, vb, fk, acc, dqt, dqs,
    part_k, rs_k, y_out, y_own, z_in, back, fin_k, tot_k,
    part_v, fin_v, acc_own, out_k, out_v, own_k, rs_v, one_k, one_v, sum_v, tot,
    lse, doc, doc_a, doc_b,
    in_sem, sib_send, sib_recv, near_send, near_recv, last_send, last_recv, one_send, one_recv,
    s_a, r_a, s_z, r_z, s_y, r_y, s_b, r_b, s_p, r_p, s_q, r_q, s_f, r_f, s_g, r_g,
):
    rows, hd = qn.shape[1], qn.shape[2]
    half = n_tp // 2
    ys = half // 2
    own = rows // n_tp
    width = own * half
    lines = rows // 128
    scale = float(hd) ** -0.5
    c = lax.axis_index("ctx")
    t = lax.axis_index("tp")
    core = t % 2
    u = t // 2
    y = u % ys
    z = u // ys
    sib = (c, t + 1 - 2 * core)
    over_z = (c, ((1 - z) * ys + y) * 2 + core)

    loads = [
        pltpu.make_async_copy(src, dst, in_sem.at[i])
        for i, (src, dst) in enumerate((
            (k_in, kb.at[0, z, y]), (v_in, vb.at[0, z, y]), (q_in, qn.at[0]), (g_in, gn.at[0]),
            (o_in, on), (lse_in, lse), (doc_in, doc),
        ))
    ]
    for load in loads:
        load.start()

    def loop(first, last, fn):
        def one(i, _):
            fn(i)
            return 0
        lax.fori_loop(first, last, one, 0)

    def down(fn):
        loop(0, steps - 1, lambda i: fn(steps - 1 - i))

    def when_sends(fn):
        def run(s):
            @pl.when(c + s < n_ctx)
            def _():
                fn(s)
        return run

    def when_has(fn):
        def run(s):
            @pl.when(c >= s)
            def _():
                fn(s)
        return run

    def remote(src, dst, send, recv, to):
        return pltpu.make_async_remote_copy(src, dst, send, recv, to, MESH)

    def await_bytes(ref, sem):
        pltpu.make_async_copy(ref, ref, sem).wait()

    def peer(j):
        v = (u + j) % half
        return v // ys, v % ys, (c, v * 2 + core)

    def y_peer(j):
        w = (y + j) % ys
        return w, (c, (z * ys + w) * 2 + core)

    barrier = pltpu.get_barrier_semaphore()

    def greet(to):
        pl.semaphore_signal(barrier, inc=1, device_id=to, device_id_type=MESH)

    greet(sib)
    loop(1, half, lambda j: greet(peer(j)[2]))
    loop(1, n_ctx, lambda j: greet(((c + j) % n_ctx, t)))

    def near_k(j):
        return remote(kb.at[0, z, y], kb.at[0, z, y], near_send.at[0], near_recv.at[0], peer(j)[2])

    def near_v(j):
        return remote(vb.at[0, z, y], vb.at[0, z, y], near_send.at[1], near_recv.at[1], peer(j)[2])

    def along_ctx(s):
        return remote(kb.at[0, z, y], kb.at[s, z, y], s_a.at[s], r_a.at[s], ((c + s) % n_ctx, t))

    def across_z(s):
        return remote(kb.at[s, z, y], kb.at[s, z, y], s_z.at[s], r_z.at[s], over_z)

    def along_y(s, j):
        return remote(kb.at[s, :, y], kb.at[s, :, y], s_y.at[s], r_y.at[s], y_peer(j)[1])

    def block_v(s):
        return remote(vb.at[0], vb.at[s], s_b.at[s], r_b.at[s], ((c + s) % n_ctx, t))

    sib_q = remote(qn.at[0], qn.at[1], sib_send.at[0], sib_recv.at[0], sib)
    sib_g = remote(gn.at[0], gn.at[1], sib_send.at[1], sib_recv.at[1], sib)
    sib_x = remote(xt.at[0, pl.ds(0, 16)], xt.at[1, pl.ds(0, 16)], sib_send.at[2], sib_recv.at[2], sib)
    sib_d = remote(dqt.at[1], dqs, sib_send.at[3], sib_recv.at[3], sib)

    for load in loads[:2]:
        load.wait()
    pl.semaphore_wait(barrier, 1 + half - 1 + n_ctx - 1)
    down(when_sends(lambda s: along_ctx(s).start()))
    loop(1, half, lambda j: near_v(j).start())
    for load in loads[2:4]:
        load.wait()
    sib_q.start()
    sib_g.start()
    loop(1, half, lambda j: near_k(j).start())
    for load in loads[4:]:
        load.wait()
    q_doc = jnp.concatenate([doc[pl.ds(c * lines + j, 1), :] for j in range(lines)], axis=1)
    delta = jnp.sum(gn[0].T.astype(F32) * on[...].T.astype(F32), axis=0, keepdims=True)
    place = lax.broadcasted_iota(jnp.int32, (8, rows), 0)
    extra = jnp.zeros((8, rows), F32)
    for i, row in enumerate((*split3(lse[...] * math.sqrt(hd)), *split3(delta))):
        extra = jnp.where(place == i, -row, extra)
    xt[0, 0:16, :] = jnp.concatenate([jnp.where(place == q_doc, -FAR, 0.0), extra], axis=0).astype(BF16)

    sib_x.start()

    qt[0] = qn[0].T
    gt[0] = gn[0].T
    for h in range(2):
        xt[h, 16:, :] = jnp.zeros((hd - 16, rows), BF16)
    dqt[...] = jnp.zeros_like(dqt)
    turned = pltpu.roll(doc[...], 64, 1)
    doc_a[...] = jnp.where(core == 0, doc[...], turned)
    doc_b[...] = jnp.where(core == 0, turned, doc[...])
    lane = lax.broadcasted_iota(jnp.int32, (128, 128), 1)

    def features(s):
        for m in range(lines // 2):
            at = (c - s) * lines + 2 * m
            both = jnp.where(lane < 64, doc_a[pl.ds(at, 1), :], doc_b[pl.ds(at + 1, 1), :])
            other = jnp.where((lane < 11) & (both.T != lane), 1.0, 0.0)
            fk[s, m * 128:(m + 1) * 128, :] = other.astype(BF16)

    features(0)
    down(when_has(lambda s: along_ctx(s).wait_recv()))
    down(when_has(lambda s: across_z(s).start()))
    sib_x.wait_recv()
    sib_q.wait_recv()
    sib_g.wait_recv()
    qt[1] = qn[1].T
    gt[1] = gn[1].T

    await_bytes(rs_v, near_recv.at[1])

    def spread_y(s):
        across_z(s).wait_recv()
        loop(1, ys, lambda j: along_y(s, j).start())

    ahead = 2

    def wave_v(s):
        @pl.when((c + s + ahead < n_ctx) & (s + ahead < steps))
        def _():
            block_v(s + ahead).wait_send()
        block_v(s).start()

    lead = max(steps - 1 - ahead, 0)
    loop(0, steps - 1 - lead, lambda i: when_sends(wave_v)(steps - 1 - i))
    down(when_has(spread_y))
    down(when_has(features))
    await_bytes(rs_v, near_recv.at[0])

    v_lane = lax.broadcasted_iota(jnp.int32, (1, 128), 1)
    v_row = jnp.where((v_lane >= 11) & (v_lane < 14), 1.0, 0.0).astype(BF16)

    def tile(h, s, q0, tq, k0, tk, diagonal, sums):
        qs, ks = pl.ds(q0, tq), pl.ds(k0, tk)
        x = xt[h, :, qs]
        k_own = kb[s].reshape(width, hd)[k0:k0 + tk]
        v_own = vb[s].reshape(width, hd)[k0:k0 + tk]
        k_all = jnp.concatenate([k_own, fk[s, ks]], axis=1)
        v_all = jnp.concatenate([v_own, jnp.broadcast_to(v_row, (tk, 128))], axis=1)
        prob = jnp.exp2(dot(k_all, jnp.concatenate([qt[h, :, qs], x], axis=0)) * (scale * math.log2(math.e)))
        if diagonal:
            r = k0 + lax.broadcasted_iota(jnp.int32, (tk, tq), 0)
            k_pos = (r // own * 2 + core) * own + r % own
            prob = jnp.where(k_pos <= q0 + lax.broadcasted_iota(jnp.int32, (tk, tq), 1), prob, 0.0)
        dprob = dot(v_all, jnp.concatenate([gt[h, :, qs], x], axis=0))
        low = prob.astype(BF16)
        dscore = (prob * dprob).astype(BF16)
        sums[0, ks] += dot(dscore, qn[h, qs])
        sums[1, ks] += dot(low, gn[h, qs])
        dqt[h, :, qs] += dot(k_own.T, dscore)

    def to_y(s, j):
        w, to = y_peer(j)
        return remote(part_k.at[s, :, w], rs_k.at[s, j - 1], s_p.at[s], r_p.at[s], to)

    def to_z(s):
        return remote(y_out.at[s], z_in.at[s], s_q.at[s], r_q.at[s], over_z)

    def to_owner(s):
        return remote(back.at[s], fin_k.at[s], s_f.at[s], r_f.at[s], ((c + n_ctx - s) % n_ctx, t))

    def v_to_owner(s):
        return remote(part_v.at[s], fin_v.at[s], s_g.at[s], r_g.at[s], ((c + n_ctx - s) % n_ctx, t))

    def straight(i, src, dst, j):
        pz, py, to = peer(j)
        to = ((c + n_ctx - 1) % n_ctx, to[1])
        return remote(src.at[pz, py], dst.at[j], one_send.at[i], one_recv.at[i], to)

    def hand_out(s):
        part_k[s] = acc[0].astype(BF16).reshape(2, ys, own, hd)

        @pl.when(s == 1)
        def _():
            loop(0, half, lambda j: straight(0, part_k.at[1], one_k, j).start())
            out_v[...] = acc[1].astype(BF16).reshape(2, ys, own, hd)
            loop(0, half, lambda j: straight(1, out_v, one_v, j).start())

        @pl.when(s > 1)
        def _():
            part_v[s] = acc[1].astype(BF16)
            v_to_owner(s).start()
            loop(1, ys, lambda j: to_y(s, j).start())

    def sum_y(s):
        await_bytes(rs_k.at[s], r_p.at[s])

        def total(at):
            full = part_k[s, at, y].astype(F32)
            for j in range(ys - 1):
                full += rs_k[s, j, at].astype(F32)
            return full
        y_own[s] = total(z)
        y_out[s] = total(1 - z).astype(BF16)
        to_z(s).start()

    def sum_z(s):
        to_z(s).wait_recv()
        back[s] = (y_own[s] + z_in[s].astype(F32)).astype(BF16)
        to_owner(s).start()

    tq = min(256, rows)

    def edge(h, s, sums):
        for q0 in range(0, rows, tq):
            if s == 0:
                tile(h, s, q0, tq, 0, (q0 + tq) // 2, True, sums)
            else:
                tile(h, s, q0, tq, q0 // 2, width - q0 // 2, False, sums)

    acc_own[...] = jnp.zeros_like(acc_own)
    edge(1, 0, acc_own)
    pl.when(c == 0)(lambda: sib_d.start())
    edge(0, 0, acc_own)
    out_k[...] = acc_own[0].astype(BF16).reshape(2, ys, own, hd)

    def last_k(j):
        pz, py, to = peer(j)
        return remote(out_k.at[pz, py], own_k.at[j - 1], last_send.at[0], last_recv.at[0], to)

    def last_v(j):
        pz, py, to = peer(j)
        return remote(sum_v.at[pz, py], rs_v.at[j - 1], last_send.at[1], last_recv.at[1], to)

    loop(1, half, lambda j: last_k(j).start())

    def once(s, fn):
        if isinstance(s, int) and s >= steps:
            return

        @pl.when((c >= s) & (s < steps))
        def _():
            fn(s)

    def step(s, edged):
        @pl.when(s > ahead)
        def _():
            when_sends(wave_v)(s - ahead)

        @pl.when(c >= s)
        def _():
            await_bytes(part_k.at[s, :, pl.ds(0, ys - 1)], r_y.at[s])
            block_v(s).wait_recv()
            acc[...] = jnp.zeros_like(acc)
            if edged:
                edge(1, s, acc)
            else:
                tile(1, s, 0, rows, 0, width, False, acc)
            if not isinstance(s, int) or s == 1:
                @pl.when(s == 1)
                def _():
                    sib_d.start()

        once(s + 2, sum_y)
        once(s + 3, sum_z)

        @pl.when(c >= s)
        def _():
            if edged:
                edge(0, s, acc)
            else:
                tile(0, s, 0, rows, 0, width, False, acc)
            hand_out(s)

    first = steps - 1
    if first * rows == SPAN:
        step(first, True)
        first -= 1
    loop(0, first, lambda i: step(first - i, False))

    if steps > 2:
        once(2, sum_y)
    def collect_v(s):
        v_to_owner(s).wait_recv()
        acc_own[1] += fin_v[s].astype(F32)

    def far(fn):
        loop(0, steps - 2, lambda i: fn(steps - 1 - i))

    far(when_sends(collect_v))
    sum_v[...] = acc_own[1].astype(BF16).reshape(2, ys, own, hd)
    loop(1, half, lambda j: last_v(j).start())
    once(3, sum_z)
    once(2, sum_z)

    sib_d.wait_recv()
    dq_out[...] = ((dqt[0] + dqs[...]) * scale).T.astype(BF16)

    for copy in (sib_q, sib_g, sib_x, sib_d):
        copy.wait_send()

    def sent_down(s):
        along_ctx(s).wait_send()

        @pl.when(s <= ahead)
        def _():
            block_v(s).wait_send()

    def sent_near(s):
        across_z(s).wait_send()
        await_bytes(rs_k.at[s], s_y.at[s])

    def sent_up(s):
        to_owner(s).wait_send()
        v_to_owner(s).wait_send()
        await_bytes(rs_k.at[s], s_p.at[s])
        to_z(s).wait_send()

    down(when_sends(sent_down))
    down(when_has(sent_near))
    far(when_has(sent_up))

    def collect_k(s):
        to_owner(s).wait_recv()
        tot_k[...] += fin_k[s].astype(F32)

    tot_k[...] = out_k[z, y].astype(F32)
    far(when_sends(collect_k))
    for i in range(2):
        await_bytes(rs_v, near_send.at[i])

    @pl.when(c >= 1)
    def _():
        for i in range(2):
            await_bytes(one_k, one_send.at[i])

    def gathered(i, total, mine, ahead_of):
        await_bytes(rs_v, last_recv.at[i])
        for j in range(half - 1):
            total += mine[j].astype(F32)
        tot[i] = total

        @pl.when(c + 1 < n_ctx)
        def _():
            await_bytes(one_k, one_recv.at[i])
            more = ahead_of[0].astype(F32)
            for j in range(1, half):
                more += ahead_of[j].astype(F32)
            tot[i] += more

    gathered(0, tot_k[...], own_k, one_k)
    dk_out[...] = (tot[0] * scale).astype(BF16)
    gathered(1, sum_v[z, y].astype(F32), rs_v, one_v)
    dv_out[...] = tot[1].astype(BF16)
    for i in range(2):
        await_bytes(rs_v, last_send.at[i])


def hand_over(*refs):
    half = 3
    src, dst, held, came, went = refs[:half], refs[half:2 * half], refs[2 * half:3 * half], refs[-2], refs[-1]
    pieces = [(0, pl.ds(k * (src[0].shape[0] // 4), src[0].shape[0] // 4)) for k in range(4)]
    pieces += [(i, pl.ds(0, src[i].shape[0])) for i in range(1, half)]
    loads = [pltpu.make_async_copy(src[i].at[at], held[i].at[at], came.at[n]) for n, (i, at) in enumerate(pieces)]
    stores = [pltpu.make_async_copy(held[i].at[at], dst[i].at[at], went.at[n]) for n, (i, at) in enumerate(pieces)]
    for load in loads:
        load.start()
    for load, store in zip(loads, stores):
        load.wait()
        store.start()
    for store in stores:
        store.wait()


def body(n_ctx, n_tp, queries, keys, values, outputs, out_grad, log_norm, doc_ids):
    rows, hd = queries.shape
    own = keys.shape[0]
    half = n_tp // 2
    width = own * half
    steps = min(n_ctx, -(-SPAN // rows) + 1)
    doc_ids = doc_ids.reshape(-1, 128)
    dma = pltpu.SemaphoreType.DMA
    anywhere = pl.BlockSpec(memory_space=pl.ANY)
    inside = pl.BlockSpec(memory_space=pltpu.VMEM)
    grads = pl.pallas_call(
        functools.partial(kernel, n_ctx, n_tp, steps),
        out_shape=(
            jax.ShapeDtypeStruct((rows, hd), BF16),
            jax.ShapeDtypeStruct((own, hd), BF16),
            jax.ShapeDtypeStruct((own, hd), BF16),
        ),
        in_specs=[anywhere] * 7,
        out_specs=(inside, inside, inside),
        scratch_shapes=[
            pltpu.VMEM((2, rows, hd), BF16),
            pltpu.VMEM((2, rows, hd), BF16),
            pltpu.VMEM((rows, hd), BF16),
            pltpu.VMEM((2, hd, rows), BF16),
            pltpu.VMEM((2, hd, rows), BF16),
            pltpu.VMEM((2, hd, rows), BF16),
            pltpu.VMEM((steps, 2, half // 2, own, hd), BF16),
            pltpu.VMEM((steps, 2, half // 2, own, hd), BF16),
            pltpu.VMEM((steps, width, hd), BF16),
            pltpu.VMEM((2, width, hd), F32),
            pltpu.VMEM((2, hd, rows), F32),
            pltpu.VMEM((hd, rows), F32),
            pltpu.VMEM((steps, 2, half // 2, own, hd), BF16),
            pltpu.VMEM((steps, half // 2 - 1, 2, own, hd), BF16),
            pltpu.VMEM((steps, own, hd), BF16),
            pltpu.VMEM((steps, own, hd), F32),
            pltpu.VMEM((steps, own, hd), BF16),
            pltpu.VMEM((steps, own, hd), BF16),
            pltpu.VMEM((steps, own, hd), BF16),
            pltpu.VMEM((own, hd), F32),
            pltpu.VMEM((steps, width, hd), BF16),
            pltpu.VMEM((steps, width, hd), BF16),
            pltpu.VMEM((2, width, hd), F32),
            pltpu.VMEM((2, half // 2, own, hd), BF16),
            pltpu.VMEM((2, half // 2, own, hd), BF16),
            pltpu.VMEM((half - 1, own, hd), BF16),
            pltpu.VMEM((half - 1, own, hd), BF16),
            pltpu.VMEM((half, own, hd), BF16),
            pltpu.VMEM((half, own, hd), BF16),
            pltpu.VMEM((2, half // 2, own, hd), BF16),
            pltpu.VMEM((2, own, hd), F32),
            pltpu.VMEM((1, rows), F32),
            pltpu.VMEM(doc_ids.shape, jnp.int32),
            pltpu.VMEM(doc_ids.shape, jnp.int32),
            pltpu.VMEM(doc_ids.shape, jnp.int32),
            dma((7,)), dma((4,)), dma((4,)), *[dma((2,)) for _ in range(6)],
            *[dma((steps,)) for _ in range(16)],
        ],
        compiler_params=pltpu.CompilerParams(
            collective_id=0, has_side_effects=True, vmem_limit_bytes=63 * 1024 * 1024),
    )(queries, keys, values, outputs, out_grad, log_norm, doc_ids)
    return pl.pallas_call(
        hand_over,
        out_shape=tuple(jax.ShapeDtypeStruct(x.shape, x.dtype) for x in grads),
        in_specs=[anywhere] * 3,
        out_specs=(anywhere,) * 3,
        scratch_shapes=[*[pltpu.VMEM(x.shape, x.dtype) for x in grads], dma((6,)), dma((6,))],
        compiler_params=pltpu.CompilerParams(vmem_limit_bytes=63 * 1024 * 1024),
    )(*grads)


def solution(mesh):
    return jax.shard_map(
        functools.partial(body, mesh.shape["ctx"], mesh.shape["tp"]),
        mesh=mesh,
        in_specs=(
            P("ctx", "tp"),
            P(("ctx", "tp"), None),
            P(("ctx", "tp"), None),
            P("ctx", "tp"),
            P("ctx", "tp"),
            P("tp", "ctx"),
            P(),
        ),
        out_specs=(P("ctx", "tp"), P(("ctx", "tp"), None), P(("ctx", "tp"), None)),
        check_vma=False,
    )
```

```python
import functools
import math

import jax
import jax.numpy as jnp
from jax import lax
from jax.experimental import pallas as pl
from jax.experimental.pallas import tpu as pltpu
from jax.sharding import PartitionSpec as P

MESH = pl.DeviceIdType.MESH
SPAN = 5120
FAR = 8192.0
F32 = jnp.float32
BF16 = jnp.bfloat16


def split3(x):
    hi = x.astype(BF16).astype(F32)
    mid = (x - hi).astype(BF16).astype(F32)
    return hi, mid, x - hi - mid


def dot(a, b):
    return jnp.dot(a, b, preferred_element_type=F32)


def kernel(
    n_ctx, n_tp, steps,
    q_in, k_in, v_in, o_in, g_in, lse_in, doc_in,
    dq_out, dk_out, dv_out,
    qn, gn, on, qt, gt, xt, kb, vb, fk, acc, dqt, dqs,
    part_k, rs_k, y_out, y_own, z_in, back, fin_k, tot_k,
    part_v, fin_v, acc_own, out_k, out_v, own_k, rs_v, one_k, one_v, sum_v, tot,
    lse, doc, doc_a, doc_b,
    in_sem, sib_send, sib_recv, near_send, near_recv, last_send, last_recv, one_send, one_recv,
    s_a, r_a, s_z, r_z, s_y, r_y, s_b, r_b, s_p, r_p, s_q, r_q, s_f, r_f, s_g, r_g,
):
    rows, hd = qn.shape[1], qn.shape[2]
    half = n_tp // 2
    ys = half // 2
    own = rows // n_tp
    width = own * half
    lines = rows // 128
    scale = float(hd) ** -0.5
    c = lax.axis_index("ctx")
    t = lax.axis_index("tp")
    core = t % 2
    u = t // 2
    y = u % ys
    z = u // ys
    sib = (c, t + 1 - 2 * core)
    over_z = (c, ((1 - z) * ys + y) * 2 + core)

    loads = [
        pltpu.make_async_copy(src, dst, in_sem.at[i])
        for i, (src, dst) in enumerate((
            (k_in, kb.at[0, z, y]), (v_in, vb.at[0, z, y]), (q_in, qn.at[0]), (g_in, gn.at[0]),
            (o_in, on), (lse_in, lse), (doc_in, doc),
        ))
    ]
    def loop(first, last, fn):
        def one(i, _):
            fn(i)
            return 0
        lax.fori_loop(first, last, one, 0)

    def down(fn):
        loop(0, steps - 1, lambda i: fn(steps - 1 - i))

    def when_sends(fn):
        def run(s):
            @pl.when(c + s < n_ctx)
            def _():
                fn(s)
        return run

    def when_has(fn):
        def run(s):
            @pl.when(c >= s)
            def _():
                fn(s)
        return run

    def remote(src, dst, send, recv, to):
        return pltpu.make_async_remote_copy(src, dst, send, recv, to, MESH)

    def await_bytes(ref, sem):
        pltpu.make_async_copy(ref, ref, sem).wait()

    def peer(j):
        v = (u + j) % half
        return v // ys, v % ys, (c, v * 2 + core)

    def y_peer(j):
        w = (y + j) % ys
        return w, (c, (z * ys + w) * 2 + core)

    barrier = pltpu.get_barrier_semaphore()

    def greet(to):
        pl.semaphore_signal(barrier, inc=1, device_id=to, device_id_type=MESH)

    for load in loads[:2]:
        load.start()
    loop(1, half, lambda j: greet(peer(j)[2]))
    loop(1, n_ctx, lambda j: greet(((c + j) % n_ctx, t)))
    greet(sib)
    for load in loads[2:]:
        load.start()

    def near_k(j):
        return remote(kb.at[0, z, y], kb.at[0, z, y], near_send.at[0], near_recv.at[0], peer(j)[2])

    def near_v(j):
        return remote(vb.at[0, z, y], vb.at[0, z, y], near_send.at[1], near_recv.at[1], peer(j)[2])

    def along_ctx(s):
        return remote(kb.at[0, z, y], kb.at[s, z, y], s_a.at[s], r_a.at[s], ((c + s) % n_ctx, t))

    def across_z(s):
        return remote(kb.at[s, z, y], kb.at[s, z, y], s_z.at[s], r_z.at[s], over_z)

    def along_y(s, j):
        return remote(kb.at[s, :, y], kb.at[s, :, y], s_y.at[s], r_y.at[s], y_peer(j)[1])

    def block_v(s):
        return remote(vb.at[0], vb.at[s], s_b.at[s], r_b.at[s], ((c + s) % n_ctx, t))

    sib_q = remote(qn.at[0], qn.at[1], sib_send.at[0], sib_recv.at[0], sib)
    sib_g = remote(gn.at[0], gn.at[1], sib_send.at[1], sib_recv.at[1], sib)
    sib_x = remote(xt.at[0, pl.ds(0, 16)], xt.at[1, pl.ds(0, 16)], sib_send.at[2], sib_recv.at[2], sib)
    sib_d = remote(dqt.at[1], dqs, sib_send.at[3], sib_recv.at[3], sib)

    for load in loads[:2]:
        load.wait()
    pl.semaphore_wait(barrier, 1 + half - 1 + n_ctx - 1)
    down(when_sends(lambda s: along_ctx(s).start()))
    loop(1, half, lambda j: near_v(j).start())
    for load in loads[2:4]:
        load.wait()
    sib_q.start()
    sib_g.start()
    loop(1, half, lambda j: near_k(j).start())
    for load in loads[4:]:
        load.wait()
    q_doc = jnp.concatenate([doc[pl.ds(c * lines + j, 1), :] for j in range(lines)], axis=1)
    delta = jnp.sum(gn[0].T.astype(F32) * on[...].T.astype(F32), axis=0, keepdims=True)
    place = lax.broadcasted_iota(jnp.int32, (8, rows), 0)
    extra = jnp.zeros((8, rows), F32)
    for i, row in enumerate((*split3(lse[...] * math.sqrt(hd)), *split3(delta))):
        extra = jnp.where(place == i, -row, extra)
    xt[0, 0:16, :] = jnp.concatenate([jnp.where(place == q_doc, -FAR, 0.0), extra], axis=0).astype(BF16)

    sib_x.start()

    qt[0] = qn[0].T
    gt[0] = gn[0].T
    for h in range(2):
        xt[h, 16:, :] = jnp.zeros((hd - 16, rows), BF16)
    dqt[...] = jnp.zeros_like(dqt)
    turned = pltpu.roll(doc[...], 64, 1)
    doc_a[...] = jnp.where(core == 0, doc[...], turned)
    doc_b[...] = jnp.where(core == 0, turned, doc[...])
    lane = lax.broadcasted_iota(jnp.int32, (128, 128), 1)

    def features(s):
        for m in range(lines // 2):
            at = (c - s) * lines + 2 * m
            both = jnp.where(lane < 64, doc_a[pl.ds(at, 1), :], doc_b[pl.ds(at + 1, 1), :])
            other = jnp.where((lane < 11) & (both.T != lane), 1.0, 0.0)
            fk[s, m * 128:(m + 1) * 128, :] = other.astype(BF16)

    features(0)
    down(when_has(lambda s: along_ctx(s).wait_recv()))
    down(when_has(lambda s: across_z(s).start()))
    sib_x.wait_recv()
    sib_q.wait_recv()
    sib_g.wait_recv()
    qt[1] = qn[1].T
    gt[1] = gn[1].T

    await_bytes(rs_v, near_recv.at[1])

    def spread_y(s):
        across_z(s).wait_recv()
        loop(1, ys, lambda j: along_y(s, j).start())

    ahead = 2

    def wave_v(s):
        @pl.when((c + s + ahead < n_ctx) & (s + ahead < steps))
        def _():
            block_v(s + ahead).wait_send()
        block_v(s).start()

    lead = max(steps - 1 - ahead, 0)
    loop(0, steps - 1 - lead, lambda i: when_sends(wave_v)(steps - 1 - i))
    down(when_has(spread_y))
    down(when_has(features))
    await_bytes(rs_v, near_recv.at[0])

    v_lane = lax.broadcasted_iota(jnp.int32, (1, 128), 1)
    v_row = jnp.where((v_lane >= 11) & (v_lane < 14), 1.0, 0.0).astype(BF16)

    def tile(h, s, q0, tq, k0, tk, diagonal, sums):
        qs, ks = pl.ds(q0, tq), pl.ds(k0, tk)
        x = xt[h, :, qs]
        k_own = kb[s].reshape(width, hd)[k0:k0 + tk]
        v_own = vb[s].reshape(width, hd)[k0:k0 + tk]
        k_all = jnp.concatenate([k_own, fk[s, ks]], axis=1)
        v_all = jnp.concatenate([v_own, jnp.broadcast_to(v_row, (tk, 128))], axis=1)
        prob = jnp.exp2(dot(k_all, jnp.concatenate([qt[h, :, qs], x], axis=0)) * (scale * math.log2(math.e)))
        if diagonal:
            r = k0 + lax.broadcasted_iota(jnp.int32, (tk, tq), 0)
            k_pos = (r // own * 2 + core) * own + r % own
            prob = jnp.where(k_pos <= q0 + lax.broadcasted_iota(jnp.int32, (tk, tq), 1), prob, 0.0)
        dprob = dot(v_all, jnp.concatenate([gt[h, :, qs], x], axis=0))
        low = prob.astype(BF16)
        dscore = (prob * dprob).astype(BF16)
        sums[0, ks] += dot(dscore, qn[h, qs])
        sums[1, ks] += dot(low, gn[h, qs])
        dqt[h, :, qs] += dot(k_own.T, dscore)

    def to_y(s, j):
        w, to = y_peer(j)
        return remote(part_k.at[s, :, w], rs_k.at[s, j - 1], s_p.at[s], r_p.at[s], to)

    def to_z(s):
        return remote(y_out.at[s], z_in.at[s], s_q.at[s], r_q.at[s], over_z)

    def to_owner(s):
        return remote(back.at[s], fin_k.at[s], s_f.at[s], r_f.at[s], ((c + n_ctx - s) % n_ctx, t))

    def v_to_owner(s):
        return remote(part_v.at[s], fin_v.at[s], s_g.at[s], r_g.at[s], ((c + n_ctx - s) % n_ctx, t))

    def straight(i, src, dst, j):
        pz, py, to = peer(j)
        to = ((c + n_ctx - 1) % n_ctx, to[1])
        return remote(src.at[pz, py], dst.at[j], one_send.at[i], one_recv.at[i], to)

    def hand_out(s):
        part_k[s] = acc[0].astype(BF16).reshape(2, ys, own, hd)

        @pl.when(s == 1)
        def _():
            loop(0, half, lambda j: straight(0, part_k.at[1], one_k, j).start())
            out_v[...] = acc[1].astype(BF16).reshape(2, ys, own, hd)
            loop(0, half, lambda j: straight(1, out_v, one_v, j).start())

        @pl.when(s > 1)
        def _():
            part_v[s] = acc[1].astype(BF16)
            v_to_owner(s).start()
            loop(1, ys, lambda j: to_y(s, j).start())

    def sum_y(s):
        await_bytes(rs_k.at[s], r_p.at[s])

        def total(at):
            full = part_k[s, at, y].astype(F32)
            for j in range(ys - 1):
                full += rs_k[s, j, at].astype(F32)
            return full
        y_own[s] = total(z)
        y_out[s] = total(1 - z).astype(BF16)
        to_z(s).start()

    def sum_z(s):
        to_z(s).wait_recv()
        back[s] = (y_own[s] + z_in[s].astype(F32)).astype(BF16)
        to_owner(s).start()

    tq = min(256, rows)

    def edge(h, s, sums):
        for q0 in range(0, rows, tq):
            if s == 0:
                tile(h, s, q0, tq, 0, (q0 + tq) // 2, True, sums)
            else:
                tile(h, s, q0, tq, q0 // 2, width - q0 // 2, False, sums)

    acc_own[...] = jnp.zeros_like(acc_own)
    edge(1, 0, acc_own)
    pl.when(c == 0)(lambda: sib_d.start())
    edge(0, 0, acc_own)
    out_k[...] = acc_own[0].astype(BF16).reshape(2, ys, own, hd)

    def last_k(j):
        pz, py, to = peer(j)
        return remote(out_k.at[pz, py], own_k.at[j - 1], last_send.at[0], last_recv.at[0], to)

    def last_v(j):
        pz, py, to = peer(j)
        return remote(sum_v.at[pz, py], rs_v.at[j - 1], last_send.at[1], last_recv.at[1], to)

    loop(1, half, lambda j: last_k(j).start())

    def once(s, fn):
        if isinstance(s, int) and s >= steps:
            return

        @pl.when((c >= s) & (s < steps))
        def _():
            fn(s)

    def step(s, edged):
        @pl.when(s > ahead)
        def _():
            when_sends(wave_v)(s - ahead)

        @pl.when(c >= s)
        def _():
            await_bytes(part_k.at[s, :, pl.ds(0, ys - 1)], r_y.at[s])
            block_v(s).wait_recv()
            acc[...] = jnp.zeros_like(acc)
            if edged:
                edge(1, s, acc)
            else:
                tile(1, s, 0, rows, 0, width, False, acc)
            if not isinstance(s, int) or s == 1:
                @pl.when(s == 1)
                def _():
                    sib_d.start()

        once(s + 2, sum_y)
        once(s + 3, sum_z)

        @pl.when(c >= s)
        def _():
            if edged:
                edge(0, s, acc)
            else:
                tile(0, s, 0, rows, 0, width, False, acc)
            hand_out(s)

    first = steps - 1
    if first * rows == SPAN:
        step(first, True)
        first -= 1
    loop(0, first, lambda i: step(first - i, False))

    if steps > 2:
        once(2, sum_y)
    def collect_v(s):
        v_to_owner(s).wait_recv()
        acc_own[1] += fin_v[s].astype(F32)

    def far(fn):
        loop(0, steps - 2, lambda i: fn(steps - 1 - i))

    far(when_sends(collect_v))
    sum_v[...] = acc_own[1].astype(BF16).reshape(2, ys, own, hd)
    loop(1, half, lambda j: last_v(j).start())
    once(3, sum_z)
    once(2, sum_z)

    sib_d.wait_recv()
    dq_out[...] = ((dqt[0] + dqs[...]) * scale).T.astype(BF16)

    for copy in (sib_q, sib_g, sib_x, sib_d):
        copy.wait_send()

    def sent_down(s):
        along_ctx(s).wait_send()

        @pl.when(s <= ahead)
        def _():
            block_v(s).wait_send()

    def sent_near(s):
        across_z(s).wait_send()
        await_bytes(rs_k.at[s], s_y.at[s])

    def sent_up(s):
        to_owner(s).wait_send()
        v_to_owner(s).wait_send()
        await_bytes(rs_k.at[s], s_p.at[s])
        to_z(s).wait_send()

    down(when_sends(sent_down))
    down(when_has(sent_near))
    far(when_has(sent_up))

    def collect_k(s):
        to_owner(s).wait_recv()
        tot_k[...] += fin_k[s].astype(F32)

    tot_k[...] = out_k[z, y].astype(F32)
    far(when_sends(collect_k))
    for i in range(2):
        await_bytes(rs_v, near_send.at[i])

    @pl.when(c >= 1)
    def _():
        for i in range(2):
            await_bytes(one_k, one_send.at[i])

    def gathered(i, total, mine, ahead_of):
        await_bytes(rs_v, last_recv.at[i])
        for j in range(half - 1):
            total += mine[j].astype(F32)
        tot[i] = total

        @pl.when(c + 1 < n_ctx)
        def _():
            await_bytes(one_k, one_recv.at[i])
            more = ahead_of[0].astype(F32)
            for j in range(1, half):
                more += ahead_of[j].astype(F32)
            tot[i] += more

    gathered(0, tot_k[...], own_k, one_k)
    dk_out[...] = (tot[0] * scale).astype(BF16)
    gathered(1, sum_v[z, y].astype(F32), rs_v, one_v)
    dv_out[...] = tot[1].astype(BF16)
    for i in range(2):
        await_bytes(rs_v, last_send.at[i])


def hand_over(*refs):
    half = 3
    src, dst, held, came, went = refs[:half], refs[half:2 * half], refs[2 * half:3 * half], refs[-2], refs[-1]
    pieces = [(0, pl.ds(k * (src[0].shape[0] // 4), src[0].shape[0] // 4)) for k in range(4)]
    pieces += [(i, pl.ds(0, src[i].shape[0])) for i in range(1, half)]
    loads = [pltpu.make_async_copy(src[i].at[at], held[i].at[at], came.at[n]) for n, (i, at) in enumerate(pieces)]
    stores = [pltpu.make_async_copy(held[i].at[at], dst[i].at[at], went.at[n]) for n, (i, at) in enumerate(pieces)]
    for load in loads:
        load.start()
    for load, store in zip(loads, stores):
        load.wait()
        store.start()
    for store in stores:
        store.wait()


def body(n_ctx, n_tp, queries, keys, values, outputs, out_grad, log_norm, doc_ids):
    rows, hd = queries.shape
    own = keys.shape[0]
    half = n_tp // 2
    width = own * half
    steps = min(n_ctx, -(-SPAN // rows) + 1)
    doc_ids = doc_ids.reshape(-1, 128)
    dma = pltpu.SemaphoreType.DMA
    anywhere = pl.BlockSpec(memory_space=pl.ANY)
    inside = pl.BlockSpec(memory_space=pltpu.VMEM)
    grads = pl.pallas_call(
        functools.partial(kernel, n_ctx, n_tp, steps),
        out_shape=(
            jax.ShapeDtypeStruct((rows, hd), BF16),
            jax.ShapeDtypeStruct((own, hd), BF16),
            jax.ShapeDtypeStruct((own, hd), BF16),
        ),
        in_specs=[anywhere] * 7,
        out_specs=(inside, inside, inside),
        scratch_shapes=[
            pltpu.VMEM((2, rows, hd), BF16),
            pltpu.VMEM((2, rows, hd), BF16),
            pltpu.VMEM((rows, hd), BF16),
            pltpu.VMEM((2, hd, rows), BF16),
            pltpu.VMEM((2, hd, rows), BF16),
            pltpu.VMEM((2, hd, rows), BF16),
            pltpu.VMEM((steps, 2, half // 2, own, hd), BF16),
            pltpu.VMEM((steps, 2, half // 2, own, hd), BF16),
            pltpu.VMEM((steps, width, hd), BF16),
            pltpu.VMEM((2, width, hd), F32),
            pltpu.VMEM((2, hd, rows), F32),
            pltpu.VMEM((hd, rows), F32),
            pltpu.VMEM((steps, 2, half // 2, own, hd), BF16),
            pltpu.VMEM((steps, half // 2 - 1, 2, own, hd), BF16),
            pltpu.VMEM((steps, own, hd), BF16),
            pltpu.VMEM((steps, own, hd), F32),
            pltpu.VMEM((steps, own, hd), BF16),
            pltpu.VMEM((steps, own, hd), BF16),
            pltpu.VMEM((steps, own, hd), BF16),
            pltpu.VMEM((own, hd), F32),
            pltpu.VMEM((steps, width, hd), BF16),
            pltpu.VMEM((steps, width, hd), BF16),
            pltpu.VMEM((2, width, hd), F32),
            pltpu.VMEM((2, half // 2, own, hd), BF16),
            pltpu.VMEM((2, half // 2, own, hd), BF16),
            pltpu.VMEM((half - 1, own, hd), BF16),
            pltpu.VMEM((half - 1, own, hd), BF16),
            pltpu.VMEM((half, own, hd), BF16),
            pltpu.VMEM((half, own, hd), BF16),
            pltpu.VMEM((2, half // 2, own, hd), BF16),
            pltpu.VMEM((2, own, hd), F32),
            pltpu.VMEM((1, rows), F32),
            pltpu.VMEM(doc_ids.shape, jnp.int32),
            pltpu.VMEM(doc_ids.shape, jnp.int32),
            pltpu.VMEM(doc_ids.shape, jnp.int32),
            dma((7,)), dma((4,)), dma((4,)), *[dma((2,)) for _ in range(6)],
            *[dma((steps,)) for _ in range(16)],
        ],
        compiler_params=pltpu.CompilerParams(
            collective_id=0, has_side_effects=True, vmem_limit_bytes=63 * 1024 * 1024),
    )(queries, keys, values, outputs, out_grad, log_norm, doc_ids)
    return pl.pallas_call(
        hand_over,
        out_shape=tuple(jax.ShapeDtypeStruct(x.shape, x.dtype) for x in grads),
        in_specs=[anywhere] * 3,
        out_specs=(anywhere,) * 3,
        scratch_shapes=[*[pltpu.VMEM(x.shape, x.dtype) for x in grads], dma((6,)), dma((6,))],
        compiler_params=pltpu.CompilerParams(vmem_limit_bytes=63 * 1024 * 1024),
    )(*grads)


def solution(mesh):
    return jax.shard_map(
        functools.partial(body, mesh.shape["ctx"], mesh.shape["tp"]),
        mesh=mesh,
        in_specs=(
            P("ctx", "tp"),
            P(("ctx", "tp"), None),
            P(("ctx", "tp"), None),
            P("ctx", "tp"),
            P("ctx", "tp"),
            P("tp", "ctx"),
            P(),
        ),
        out_specs=(P("ctx", "tp"), P(("ctx", "tp"), None), P(("ctx", "tp"), None)),
        check_vma=False,
    )
```
